32 devices in a mesh: slot: 8 (over z, y), hid: 4 (over x, core).
Axes of the slice: x: 2, y: 2, z: 4, core: 2. Of those that a mesh axis runs over, the one named last changes fastest.
Arguments:
- master: float32 [4, 3, 4, 393216], P(None, None, 'hid', 'slot'), may hold values from -0.125 to 0.125
- first_moment: float32 [4, 3, 4, 393216], P(None, None, 'hid', 'slot'), may hold values from -0.3 to 0.3
- second_moment: float32 [4, 3, 4, 393216], P(None, None, 'hid', 'slot'), may hold values from 0.0001 to 0.01
- slot_weights: bfloat16 [8, 3, 768, 2048], P('slot', None, 'hid'), may hold values from -0.125 to 0.125
- back_rows: bfloat16 [8, 1024, 2048], P('slot'), may hold values from -6 to 6
- readout: bfloat16 [8, 1024, 2048], P('slot'), may hold values from -0.25 to 0.25
- ref_logratio: float32 [8, 1024], P('slot'), may hold values from -9 to 0
- labels: int32 [8, 1024], P('slot'), may hold values 0 or 1
- place_cur: int32 [8], replicated, may hold values from 0 to 3, as said below
- place_next: int32 [8], replicated, may hold values from 0 to 3, as said below
- fwd_rows: bfloat16 [2048, 2048], P('slot', 'hid'), may hold values from -6 to 6
- routes: int32 [2048, 1], P('slot'), may hold values from 0 to 7; in each aligned block of 256 rows (0 to 255, 256 to 511, ...) at most 64 rows name the same one
Outputs:
- out_rows: bfloat16 [2048, 2048], P('slot', 'hid')
- new_master: float32 [4, 3, 4, 393216], P(None, None, 'hid', 'slot')
- new_first: float32 [4, 3, 4, 393216], P(None, None, 'hid', 'slot')
- new_second: float32 [4, 3, 4, 393216], P(None, None, 'hid', 'slot')
The draws below stay inside these ranges and needn't reach their ends.
Inputs may be any that keep to these rules, and one draw needn't show every extreme that they name: `place_cur`: every expert 0 to 3 is held by at least one slot. `place_next`: every expert 0 to 3 is held by at least one slot. `routes`: the rows of one slot name any one slot at most 64 times, a bound that some block reaches.
All inputs are finite; a program needn't handle non-finite values. No bound on the sum of `labels` on one device may be relied on, other than what follows from the above.
Results may differ from the reference program's by a relative error of at most 0.008.
Values may be sent and summed in bfloat16 or wider, within the bound.
A program may use at most 128 MiB of HBM per device.

```python
import math
import jax
import jax.numpy as jnp
import numpy as np
from jax import lax

D = 2048
FF = 768
ROWS_B = 1024
ROWS_F = 256
SLOTS = 8
EXPERTS = 4
CAP = 64
N_HID = 4


def placement_draw(key):
    spare_slots = SLOTS - EXPERTS
    key_list = jax.random.split(key, 4)
    first_pick = jax.random.randint(key_list[0], (spare_slots,), 0, EXPERTS)
    second_pick = jax.random.randint(key_list[1], (spare_slots,), 0, EXPERTS)
    relabel = jax.random.permutation(key_list[2], EXPERTS)
    chosen = relabel[jnp.minimum(first_pick, second_pick)].astype(jnp.int32)
    listed = jnp.concatenate([jnp.arange(EXPERTS, dtype=jnp.int32), chosen])
    shuffle = jax.random.permutation(key_list[3], SLOTS)
    return listed[shuffle].astype(jnp.int32)


def draw_place_cur(key, part):
    return placement_draw(jax.random.fold_in(key, 11))


def draw_place_next(key, part):
    return placement_draw(jax.random.fold_in(key, 23))


def draw_ref_logratio(key, part):
    inner_key = jax.random.fold_in(key, 37)
    ramp = 1.0 + 2.0 * jnp.arange(SLOTS, dtype=jnp.float32)[:, None] / max(SLOTS - 1, 1)
    rough = jax.random.uniform(inner_key, (SLOTS, ROWS_B), jnp.float32, 0.5, 1.5)
    return (-0.5 * ramp * rough).astype(jnp.float32)


def plant(result, stream_key, smallest, high):
    shape = result.shape
    spot = [jax.random.randint(jax.random.fold_in(stream_key, axis), (), 0, shape[axis]) for axis in range(len(shape))]
    result = result.at[tuple(spot)].set(smallest)
    longest = shape.index(max(shape))
    spot[longest] = (spot[longest] + 1) % shape[longest]
    return result.at[tuple(spot)].set(high)


def shard_levels(rng, extent, cuts, least, top_value):
    factor_of, own = 1.0, jax.random.fold_in(rng, 6)
    for position, parts in cuts:
        steps = jnp.exp(jax.random.uniform(jax.random.fold_in(own, position), (parts,), jnp.float32, least / len(cuts), top_value / len(cuts)))
        factor_of = factor_of * jnp.repeat(steps, extent[position] // parts).reshape([-1 if axis == position else 1 for axis in range(len(extent))])
    return factor_of


def shared_out(rng, own, number, rows, amount, top, most, skew):
    sequence = jax.random.permutation(rng, amount)
    crowded, usual = shares(amount, rows * top, most, skew, True), shares(amount, rows * top, most, skew, False)
    places = jnp.arange(amount)

    def named(sizes, turn):
        used = int((sizes > 0).sum())
        fixed = max(1, used // 4)
        shifted = fixed + (places - fixed + turn * (used - fixed)) % max(1, amount - fixed)
        return jnp.zeros((amount,), jnp.int32).at[sequence[jnp.where(places < fixed, places, shifted)]].set(jnp.asarray(sizes, jnp.int32))

    sizes = jnp.where(number % 4 == 0, named(crowded, number // 4), named(usual, number - number // 4 - 1))
    mixed = jax.random.permutation(jax.random.fold_in(own, 3), amount)
    giver, receiver = mixed[0:amount // 2 * 2:2], mixed[1:amount // 2 * 2:2]
    margin = jnp.minimum(sizes[giver] - 1, most - sizes[receiver]) // 2
    margin = jnp.where((giver == sequence[0]) | (receiver == sequence[0]) | (sizes[receiver] == 0), 0, jnp.maximum(margin, 0))
    shifted = jax.random.randint(jax.random.fold_in(own, 4), (amount // 2,), 0, 1 << 20) % (margin + 1)
    sizes = sizes.at[giver].add(-shifted).at[receiver].add(shifted)
    members = jnp.searchsorted(jnp.cumsum(sizes), jnp.arange(rows * top), side="right").astype(jnp.int32)
    table = members.reshape(top, rows).T
    table = table[jax.random.permutation(jax.random.fold_in(own, 1), rows)]
    turn = jax.random.randint(jax.random.fold_in(own, 2), (rows, 1), 0, top)
    return jnp.take_along_axis(table, (jnp.arange(top)[None, :] + turn) % top, axis=1)


def shares(number_of, total, bound, lean, full):
    loads = [(1 << 20) // math.isqrt(grade ** lean) + 1 for grade in range(1, number_of + 1)]
    largest = bound if full else min(bound, max(-(-total // number_of), total * loads[0] // sum(loads)))
    least = 1 if total - largest >= number_of - 1 else 0
    given, spare = [largest] + [least] * (number_of - 1), total - largest - least * (number_of - 1)
    while spare > 0:
        candidates = [i for i in range(1, number_of) if given[i] < largest] or [i for i in range(1, number_of) if given[i] < bound]
        whole, left = sum([loads[i] for i in candidates]), spare
        for i in candidates:
            extra = min(bound - given[i], max(1, left * loads[i] // whole), spare)
            given[i] = given[i] + extra
            spare = spare - extra
    return np.array(given)


def bell_draw(own_key, dims, width, reach, shards=(), held_as=jnp.bfloat16):
    level = shard_levels(own_key, dims, shards, -0.22, 0.18) if shards else 1.0
    result = jax.random.normal(own_key, dims, jnp.float32) * width * level
    return jnp.minimum(jnp.maximum(result, -reach), reach).astype(held_as)


def setup_inputs(seed: int = 0) -> dict:
    streams_of = jax.random.split(jax.random.key(seed), 13)
    master = bell_draw(streams_of[0], (EXPERTS, 3, N_HID, FF * D // N_HID), D ** -0.5, 0.125, ((2, 4), (3, 8)), jnp.float32)
    first_moment = bell_draw(streams_of[1], (EXPERTS, 3, N_HID, FF * D // N_HID), 0.05, 0.3, ((2, 4), (3, 8)), jnp.float32)
    second_moment = jnp.clip(jnp.exp(math.log(0.01) - 4.6051702 * jax.random.uniform(streams_of[2], (EXPERTS, 3, N_HID, FF * D // N_HID), jnp.float32) ** shard_levels(streams_of[2], (EXPERTS, 3, N_HID, FF * D // N_HID), ((2, 4), (3, 8)), -0.2, 0.2)), 0.0001, 0.01)
    slot_weights = bell_draw(streams_of[3], (SLOTS, 3, FF, D), D ** -0.5, 0.125, ((0, 8), (2, 4)))
    back_rows = bell_draw(streams_of[4], (SLOTS, ROWS_B, D), 1.0, 6.0, ((0, 8),))
    readout = bell_draw(streams_of[5], (SLOTS, ROWS_B, D), (D // 4) ** -0.5, 0.25, ((0, 8),))
    ref_logratio = draw_ref_logratio(jax.random.fold_in(streams_of[12], 71), 0)
    labels = plant((jax.random.randint(streams_of[7], (SLOTS, ROWS_B), 0, 2) < 1).astype(jnp.int32), jax.random.fold_in(streams_of[7], 1), 0, 1)
    place_cur = draw_place_cur(jax.random.fold_in(streams_of[12], 71), 0)
    place_next = draw_place_next(jax.random.fold_in(streams_of[12], 71), 0)
    fwd_rows = bell_draw(streams_of[10], (SLOTS * ROWS_F, D), 1.0, 6.0, ((0, 8), (1, 4)))
    routes_keys = jax.random.split(jax.random.fold_in(streams_of[11], 1), (SLOTS * ROWS_F) // ROWS_F)
    routes_turns = jax.random.permutation(jax.random.fold_in(streams_of[11], 3), (SLOTS * ROWS_F) // ROWS_F)
    routes = jax.vmap(lambda own, number: shared_out(jax.random.fold_in(streams_of[11], 2), own, number, ROWS_F, SLOTS, 1, CAP, 2))(routes_keys, routes_turns).reshape((SLOTS * ROWS_F, 1))
    return {"master": master, "first_moment": first_moment, "second_moment": second_moment, "slot_weights": slot_weights, "back_rows": back_rows, "readout": readout, "ref_logratio": ref_logratio, "labels": labels, "place_cur": place_cur, "place_next": place_next, "fwd_rows": fwd_rows, "routes": routes}


beta_kto = 1.0
desired_weight = 1.0
undesired_weight = 1.33
learn_rate = 0.004
decay_first = 0.9
decay_second = 0.999
correct_first = 0.9999734386011124
correct_second = 0.09520785288629043
adam_eps = 1e-08
weight_decay = 0.1

def expert_pass(inputs, weights):
    across = (((1,), (1,)), ((), ()))
    gate_vals = lax.dot_general(inputs, weights[0], across, preferred_element_type=jnp.float32)
    up_vals = lax.dot_general(inputs, weights[1], across, preferred_element_type=jnp.float32)
    hidden = (gate_vals * jax.nn.sigmoid(gate_vals) * up_vals).astype(jnp.bfloat16)
    produced = jnp.dot(hidden, weights[2], preferred_element_type=jnp.float32)
    return (gate_vals, up_vals, hidden, produced)

def kto_slope(scores, labels, center):
    sigma_v = jax.nn.sigmoid(beta_kto * (scores - center))
    signed = jnp.where(labels == 1, -desired_weight, undesired_weight)
    return beta_kto * sigma_v * (1.0 - sigma_v) * signed

def expert_grads(inputs, direction, weights, slope):
    gate_vals, up_vals, hidden, _ = expert_pass(inputs, weights)
    d_expert = (slope[:, None] * direction.astype(jnp.float32)).astype(jnp.bfloat16)
    d_hidden = lax.dot_general(d_expert, weights[2], (((1,), (1,)), ((), ())), preferred_element_type=jnp.float32)
    sigma_g = jax.nn.sigmoid(gate_vals)
    d_gate = (d_hidden * up_vals * sigma_g * (1.0 + gate_vals * (1.0 - sigma_g))).astype(jnp.bfloat16)
    d_up = (d_hidden * gate_vals * sigma_g).astype(jnp.bfloat16)
    contract = (((0,), (0,)), ((), ()))
    grad_gate = lax.dot_general(d_gate, inputs, contract, preferred_element_type=jnp.float32)
    grad_up = lax.dot_general(d_up, inputs, contract, preferred_element_type=jnp.float32)
    grad_down = lax.dot_general(hidden, d_expert, contract, preferred_element_type=jnp.float32)
    return jnp.stack([grad_gate, grad_up, grad_down])

def adamw_update(master, first_moment, second_moment, summed):
    new_first = decay_first * first_moment + (1.0 - decay_first) * summed
    new_second = decay_second * second_moment + (1.0 - decay_second) * summed * summed
    update = new_first / correct_first / (jnp.sqrt(new_second / correct_second) + adam_eps)
    new_master = master - learn_rate * (update + weight_decay * master)
    return (new_master, new_first, new_second)

def reference(master, first_moment, second_moment, slot_weights, back_rows, readout, ref_logratio, labels, place_cur, place_next, fwd_rows, routes):

    def policy_terms(packed):
        inputs, direction, weights = packed
        produced = expert_pass(inputs, weights)[3]
        return lax.optimization_barrier(jnp.sum(produced * direction.astype(jnp.float32), axis=1))
    policy = lax.map(policy_terms, (back_rows, readout, slot_weights))
    scores = policy - ref_logratio
    center = jnp.mean(scores)
    slope = kto_slope(scores, labels, center)

    def accumulate(running, packed):
        inputs, direction, weights, slope_row, expert_id = packed
        grads = expert_grads(inputs, direction, weights, slope_row)
        return (running.at[expert_id].add(grads), None)
    start_sum = jnp.zeros((EXPERTS, 3, FF, D), jnp.float32)
    summed, _ = lax.scan(accumulate, start_sum, (back_rows, readout, slot_weights, slope, place_cur))
    summed = summed.reshape(master.shape)
    new_master, new_first, new_second = adamw_update(master, first_moment, second_moment, summed)
    next_weights = new_master.astype(jnp.bfloat16).reshape(EXPERTS, 3, FF, D)[place_next]
    target = routes[:, 0].astype(jnp.int32)
    total_rows = target.shape[0]
    span = SLOTS * CAP
    sort_order = jnp.argsort(target, stable=True).astype(jnp.int32)
    sorted_rows = jnp.concatenate([fwd_rows[sort_order], jnp.zeros((span, D), jnp.bfloat16)], axis=0)
    counts = lax.optimization_barrier(jnp.sum((target[:, None] == jnp.arange(SLOTS, dtype=jnp.int32)[None, :]).astype(jnp.int32), axis=0))
    starts = (jnp.cumsum(counts) - counts).astype(jnp.int32)

    def apply_slot(packed):
        weights, start_at = packed
        block_rows = lax.dynamic_slice_in_dim(sorted_rows, start_at, span, 0)
        return expert_pass(block_rows, weights)[3].astype(jnp.bfloat16)
    results = lax.map(apply_slot, (next_weights, starts))
    sorted_target = target[sort_order]
    within = (jnp.arange(total_rows, dtype=jnp.int32) - starts[sorted_target]).astype(jnp.int32)
    ordered_out = results[sorted_target, within]
    out_rows = jnp.zeros((total_rows, D), jnp.bfloat16).at[sort_order].set(ordered_out)
    return (out_rows, new_master, new_first, new_second)
```

```python
import functools

import jax
import jax.numpy as jnp
from jax import lax
from jax.experimental import pallas as pl
from jax.experimental.pallas import tpu as pltpu
from jax.sharding import PartitionSpec as P

beta_kto = 1.0
desired_weight = 1.0
undesired_weight = 1.33
learn_rate = 0.004
decay_first = 0.9
decay_second = 0.999
correct_first = 0.9999734386011124
correct_second = 0.09520785288629043
adam_eps = 1e-08
weight_decay = 0.1


def expert_pass(inputs, weights):
    across = (((1,), (1,)), ((), ()))
    gate_vals = lax.dot_general(inputs, weights[0], across, preferred_element_type=jnp.float32)
    up_vals = lax.dot_general(inputs, weights[1], across, preferred_element_type=jnp.float32)
    hidden = (gate_vals * jax.nn.sigmoid(gate_vals) * up_vals).astype(jnp.bfloat16)
    produced = jnp.dot(hidden, weights[2], preferred_element_type=jnp.float32)
    return (gate_vals, up_vals, hidden, produced)


def kto_slope(scores, labels, center):
    sigma_v = jax.nn.sigmoid(beta_kto * (scores - center))
    signed = jnp.where(labels == 1, -desired_weight, undesired_weight)
    return beta_kto * sigma_v * (1.0 - sigma_v) * signed


def expert_backward(inputs, direction, weights, slope, gate_vals, up_vals, hidden):
    d_expert = (slope[:, None] * direction.astype(jnp.float32)).astype(jnp.bfloat16)
    d_hidden = lax.dot_general(
        d_expert, weights[2], (((1,), (1,)), ((), ())), preferred_element_type=jnp.float32
    )
    sigma_g = jax.nn.sigmoid(gate_vals)
    d_gate = (d_hidden * up_vals * sigma_g * (1.0 + gate_vals * (1.0 - sigma_g))).astype(
        jnp.bfloat16
    )
    d_up = (d_hidden * gate_vals * sigma_g).astype(jnp.bfloat16)
    contract = (((0,), (0,)), ((), ()))
    grad_gate = lax.dot_general(d_gate, inputs, contract, preferred_element_type=jnp.float32)
    grad_up = lax.dot_general(d_up, inputs, contract, preferred_element_type=jnp.float32)
    grad_down = lax.dot_general(hidden, d_expert, contract, preferred_element_type=jnp.float32)
    return jnp.stack([grad_gate, grad_up, grad_down])


def adamw_update(master, first_moment, second_moment, summed):
    new_first = decay_first * first_moment + (1.0 - decay_first) * summed
    new_second = decay_second * second_moment + (1.0 - decay_second) * summed * summed
    update = new_first / correct_first / (jnp.sqrt(new_second / correct_second) + adam_eps)
    new_master = master - learn_rate * (update + weight_decay * master)
    return (new_master, new_first, new_second)


def shards(
    master,
    first_moment,
    second_moment,
    slot_weights,
    back_rows,
    readout,
    ref_logratio,
    labels,
    place_cur,
    place_next,
    fwd_rows,
    routes,
):
    slot_count = lax.axis_size("slot")
    experts_here = master.shape[0]
    weights = slot_weights[0]
    width = weights.shape[2]
    owned_units = master.shape[3] // width
    inputs = back_rows[0]
    direction = readout[0]
    gate_vals, up_vals, hidden, partial_value = expert_pass(inputs, weights)
    row_part = jnp.sum(partial_value * direction.astype(jnp.float32), axis=1)
    policy = lax.psum(row_part, "hid")
    scores = policy - ref_logratio[0]
    row_total = slot_count * inputs.shape[0]
    center = lax.psum(jnp.sum(scores), "slot") / row_total
    slope = kto_slope(scores, labels[0], center)
    grads = expert_backward(inputs, direction, weights, slope, gate_vals, up_vals, hidden)
    arrived = lax.all_to_all(
        grads[None].astype(jnp.bfloat16), "slot", split_axis=2, concat_axis=0, tiled=True
    ).astype(jnp.float32)
    arrived = arrived.reshape(slot_count, 3, 1, owned_units * width)
    owner_map = (place_cur[None, :] == jnp.arange(experts_here, dtype=jnp.int32)[:, None]).astype(
        jnp.float32
    )
    summed = jnp.einsum("es,sabc->eabc", owner_map, arrived, precision=lax.Precision.HIGHEST)
    new_master, new_first, new_second = adamw_update(master, first_moment, second_moment, summed)
    refreshed = new_master.astype(jnp.bfloat16)
    pick_map = (place_next[:, None] == jnp.arange(experts_here, dtype=jnp.int32)[None, :]).astype(
        jnp.bfloat16
    )
    picked = jnp.einsum(
        "se,eabc->sabc", pick_map, refreshed, preferred_element_type=jnp.float32
    ).astype(jnp.bfloat16)
    picked = picked.reshape(slot_count, 3, owned_units, width)
    resident = lax.all_to_all(picked, "slot", split_axis=0, concat_axis=2, tiled=True)[0]
    capacity = 2 * fwd_rows.shape[0] // slot_count
    quarter = fwd_rows.shape[1]
    target = routes[:, 0]
    target_map = (target[:, None] == jnp.arange(slot_count, dtype=jnp.int32)[None, :]).astype(
        jnp.int32
    )
    earlier = jnp.cumsum(target_map, axis=0) - target_map
    position = jnp.sum(earlier * target_map, axis=1)
    slot_place = target * capacity + position
    place_map = (
        slot_place[None, :] == jnp.arange(slot_count * capacity, dtype=jnp.int32)[:, None]
    ).astype(jnp.bfloat16)
    buffer_rows = jnp.dot(place_map, fwd_rows, preferred_element_type=jnp.float32).astype(
        jnp.bfloat16
    )
    buffer_rows = buffer_rows.reshape(slot_count, capacity, quarter)
    arrived_rows = lax.all_to_all(
        buffer_rows, "slot", split_axis=0, concat_axis=0, tiled=True
    ).reshape(slot_count * capacity, quarter)
    across = (((1,), (1,)), ((), ()))
    piece_rows = lax.all_gather(arrived_rows, "hid", axis=1, tiled=True)
    gate_cols = resident[0]
    up_cols = resident[1]
    fwd_gate = lax.dot_general(piece_rows, gate_cols, across, preferred_element_type=jnp.float32)
    fwd_up = lax.dot_general(piece_rows, up_cols, across, preferred_element_type=jnp.float32)
    fwd_hidden = (fwd_gate * jax.nn.sigmoid(fwd_gate) * fwd_up).astype(jnp.bfloat16)
    fwd_partial = jnp.dot(fwd_hidden, resident[2], preferred_element_type=jnp.float32)
    totals = lax.psum(fwd_partial, "hid")
    shares = lax.dynamic_slice_in_dim(totals, lax.axis_index("hid") * quarter, quarter, 1)
    outgoing = shares.astype(jnp.bfloat16).reshape(slot_count, capacity, quarter)
    returned = lax.all_to_all(outgoing, "slot", split_axis=0, concat_axis=0, tiled=True).reshape(
        slot_count * capacity, quarter
    )
    out_rows = lax.dot_general(
        place_map, returned, (((0,), (0,)), ((), ())), preferred_element_type=jnp.float32
    ).astype(jnp.bfloat16)
    return (out_rows, new_master, new_first, new_second)


ACROSS = (((1,), (1,)), ((), ()))
F32 = jnp.float32
BF16 = jnp.bfloat16
MESH = pl.DeviceIdType.MESH
ROW_STEP = 256


def kto_kernel(
    slots,
    hids,
    owned,
    experts,
    place_cur,
    place_next,
    rows_in,
    back_map,
    ref_ref,
    sign_ref,
    w_hbm,
    x_hbm,
    r_hbm,
    mast_hbm,
    mom1_hbm,
    mom2_hbm,
    out_ref,
    nmast_hbm,
    nmom1_hbm,
    nmom2_hbm,
    w_v,
    x_v,
    r_v,
    mast_v,
    mom1_v,
    mom2_v,
    pre_gate,
    pre_up,
    hid_v,
    d_gu,
    d_hid,
    gsend,
    grecv,
    wsend,
    wrecv,
    rows_full,
    part_v,
    part_all,
    tot_v,
    tot_all,
    out_part,
    lev1,
    lev2_send,
    lev2,
    ret_send,
    ret_recv,
    load_sem,
    xr_sem,
    mom_sem,
    store_sem,
    row_ss,
    row_rs,
    gat_ss,
    gat_rs,
    part_ss,
    part_rs,
    tot_ss,
    tot_rs,
    g_ss,
    g_rs,
    w_ss,
    w_rs,
    l1_ss,
    l1_rs,
    l2_ss,
    l2_rs,
    ret_ss,
    ret_rs,
):
    me_s = lax.axis_index("slot")
    me_h = lax.axis_index("hid")
    width = w_v.shape[2]
    half = width // 2
    quarter = rows_in.shape[2]
    cap = rows_in.shape[1]
    pair = 2 * owned
    rows = x_v.shape[0]
    steps = rows // ROW_STEP

    def slot_peer(k):
        return lax.rem(me_s + k, slots)

    def hid_peer(k):
        return lax.rem(me_h + k, hids)

    def remote(src, dst, ssem, rsem, slot=None, hid=None):
        return pltpu.make_async_remote_copy(
            src_ref=src,
            dst_ref=dst,
            send_sem=ssem,
            recv_sem=rsem,
            device_id=(me_s if slot is None else slot, me_h if hid is None else hid),
            device_id_type=MESH,
        )

    def loop(low, high, body):
        def step(i, carry):
            body(i)
            return carry

        lax.fori_loop(low, high, step, 0)

    w_load = pltpu.make_async_copy(w_hbm, w_v, load_sem.at[0])
    w_load.start()

    def xr_copies(c):
        at = pl.ds(pl.multiple_of(c * ROW_STEP, ROW_STEP), ROW_STEP)
        return (
            pltpu.make_async_copy(x_hbm.at[at], x_v.at[at], xr_sem.at[0, c]),
            pltpu.make_async_copy(r_hbm.at[at], r_v.at[at], xr_sem.at[1, c]),
        )

    def start_xr(c):
        for copy in xr_copies(c):
            copy.start()

    loop(0, steps, start_xr)
    state = ((mast_hbm, mast_v, nmast_hbm), (mom1_hbm, mom1_v, nmom1_hbm), (mom2_hbm, mom2_v, nmom2_hbm))
    for i, (src, dst, _) in enumerate(state):
        pltpu.make_async_copy(src, dst, mom_sem.at[i]).start()

    barrier = pltpu.get_barrier_semaphore()

    def greet_slot(k):
        pl.semaphore_signal(barrier, inc=1, device_id=(slot_peer(k), me_h), device_id_type=MESH)

    def greet_hid(k):
        pl.semaphore_signal(barrier, inc=1, device_id=(me_s, hid_peer(k)), device_id_type=MESH)

    loop(1, slots, greet_slot)
    loop(1, hids, greet_hid)
    pl.semaphore_wait(barrier, slots + hids - 2)

    def row_copy(to):
        return remote(
            rows_in.at[to], rows_full.at[me_h, me_s], row_ss.at[to], row_rs.at[me_s], slot=to
        )

    loop(1, slots, lambda k: row_copy(slot_peer(k)).start())
    rows_full[me_h, me_s] = rows_in[me_s]

    w_load.wait()

    def first_half(c):
        for copy in xr_copies(c):
            copy.wait()
        at = pl.ds(pl.multiple_of(c * ROW_STEP, ROW_STEP), ROW_STEP)
        xc = x_v[at, :]
        rc = r_v[at, :]
        gate = lax.dot_general(w_v[0], xc, ACROSS, preferred_element_type=F32)
        up = lax.dot_general(w_v[1], xc, ACROSS, preferred_element_type=F32)
        turn = lax.dot_general(w_v[2], rc, ACROSS, preferred_element_type=F32)
        sig = jax.nn.sigmoid(gate)
        act = gate * sig
        hidden = (act * up).astype(BF16).astype(F32)
        part_v[:, at] = jnp.sum(hidden * turn, axis=0, keepdims=True)
        pre_gate[:, at] = turn * up * sig * (1.0 + gate * (1.0 - sig))
        pre_up[:, at] = turn * act
        hid_v[:, at] = hidden

    loop(0, steps, first_half)

    def part_copy(to):
        return remote(part_v, part_all.at[me_h], part_ss.at[to], part_rs.at[me_h], hid=to)

    loop(1, hids, lambda k: part_copy(hid_peer(k)).start())
    part_all[me_h] = part_v[...]

    def part_wait(k):
        frm = hid_peer(k)
        remote(part_v, part_all.at[frm], part_ss.at[frm], part_rs.at[frm], hid=frm).wait_recv()

    loop(1, hids, part_wait)
    policy = part_all[0]
    for h in range(1, hids):
        policy = policy + part_all[h]
    scores = policy - ref_ref[...]
    tot_v[...] = jnp.broadcast_to(jnp.sum(scores, axis=1, keepdims=True), tot_v.shape)

    def tot_copy(to):
        return remote(tot_v, tot_all.at[me_s], tot_ss.at[to], tot_rs.at[me_s], slot=to)

    loop(1, slots, lambda k: tot_copy(slot_peer(k)).start())
    tot_all[me_s] = tot_v[...]

    def tot_wait(k):
        frm = slot_peer(k)
        remote(tot_v, tot_all.at[frm], tot_ss.at[frm], tot_rs.at[frm], slot=frm).wait_recv()

    loop(1, slots, tot_wait)
    total = tot_all[0]
    for s in range(1, slots):
        total = total + tot_all[s]
    center = total[:, :1] * (1.0 / (slots * rows))
    sigma_v = jax.nn.sigmoid(beta_kto * (scores - center))
    slope = beta_kto * sigma_v * (1.0 - sigma_v) * sign_ref[...]

    for s in range(slots):
        units = pl.ds(s * owned, owned)
        both = jnp.concatenate([pre_gate[units, :] * slope, pre_up[units, :] * slope], axis=0)
        d_gu[pl.ds(s * pair, pair), :] = both.astype(BF16)
    d_hid[...] = (hid_v[...] * slope).astype(BF16)

    def grad_copy(p, to):
        return remote(
            gsend.at[p, to], grecv.at[p, me_s], g_ss.at[p, to], g_rs.at[p, me_s], slot=to
        )

    cut = 512
    per_piece = half // cut
    for p in range(3):

        def grads(i, p=p):
            here = pl.ds(pl.multiple_of(i * cut, cut), cut)
            if p < 2:
                at = pl.ds(pl.multiple_of(p * half + i * cut, cut), cut)
                found = jnp.dot(d_gu[...], x_v[:, at], preferred_element_type=F32)
                gsend[p, :, :, here] = found.astype(BF16).reshape(slots, pair, cut)
            else:
                high = pl.ds(pl.multiple_of(half + i * cut, cut), cut)
                low_part = jnp.dot(d_hid[...], r_v[:, here], preferred_element_type=F32)
                high_part = jnp.dot(d_hid[...], r_v[:, high], preferred_element_type=F32)
                both = jnp.concatenate(
                    [low_part.reshape(slots, owned, cut), high_part.reshape(slots, owned, cut)],
                    axis=1,
                )
                gsend[p, :, :, here] = both.astype(BF16)

        loop(0, per_piece, grads)
        loop(1, slots, lambda k, p=p: grad_copy(p, slot_peer(k)).start())
        grecv[p, me_s] = gsend[p, me_s]

    def row_wait(k):
        frm = slot_peer(k)
        remote(
            rows_in.at[frm], rows_full.at[me_h, frm], row_ss.at[frm], row_rs.at[frm], slot=frm
        ).wait_recv()

    loop(1, slots, row_wait)

    def gather_copy(to):
        return remote(
            rows_full.at[me_h], rows_full.at[me_h], gat_ss.at[to], gat_rs.at[me_h], hid=to
        )

    loop(1, hids, lambda k: gather_copy(hid_peer(k)).start())

    for i, (src, dst, _) in enumerate(state):
        pltpu.make_async_copy(src, dst, mom_sem.at[i]).wait()
    cur = [place_cur[s] for s in range(slots)]
    nxt = [place_next[s] for s in range(slots)]
    is_cur = [[jnp.where(cur[s] == e, 1.0, 0.0) for s in range(slots)] for e in range(experts)]
    is_nxt = [[jnp.where(nxt[t] == e, 1.0, 0.0) for t in range(slots)] for e in range(experts)]
    blocks = width // 128
    half_blocks = half // 128

    def weight_copy(p, to):
        return remote(
            wsend.at[p, to], wrecv.at[p, me_s], w_ss.at[p, to], w_rs.at[p, me_s], slot=to
        )

    for p in range(3):

        def grad_wait(k, p=p):
            frm = slot_peer(k)
            remote(
                gsend.at[p, frm], grecv.at[p, frm], g_ss.at[p, frm], g_rs.at[p, frm], slot=frm
            ).wait_recv()

        loop(1, slots, grad_wait)

        def adam(j, p=p):
            lanes = pl.ds(pl.multiple_of(j * 128, 128), 128)
            came = [grecv[p, s, :, lanes].astype(F32) for s in range(slots)]
            fresh = []
            for e in range(experts):
                summed = came[0] * is_cur[e][0]
                for s in range(1, slots):
                    summed = summed + came[s] * is_cur[e][s]
                sides = []
                for side in range(2):
                    if p < 2:
                        row, block = e * 3 + side, p * half_blocks + j
                    else:
                        row, block = e * 3 + 2, side * half_blocks + j
                    at = pl.ds(block, owned, stride=blocks)
                    new_m, new_1, new_2 = adamw_update(
                        mast_v[row, at, :],
                        mom1_v[row, at, :],
                        mom2_v[row, at, :],
                        summed[side * owned : (side + 1) * owned],
                    )
                    mast_v[row, at, :] = new_m
                    mom1_v[row, at, :] = new_1
                    mom2_v[row, at, :] = new_2
                    sides.append(new_m)
                fresh.append(jnp.concatenate(sides, axis=0))
            for t in range(slots):
                chosen = fresh[0] * is_nxt[0][t]
                for e in range(1, experts):
                    chosen = chosen + fresh[e] * is_nxt[e][t]
                wsend[p, t, :, lanes] = chosen.astype(BF16)

        loop(0, half_blocks, adam)
        loop(1, slots, lambda k, p=p: weight_copy(p, slot_peer(k)).start())
        wrecv[p, me_s] = wsend[p, me_s]
    for i, (_, dst, new) in enumerate(state):
        pltpu.make_async_copy(dst, new, store_sem.at[i]).start()

    def gather_wait(k):
        frm = hid_peer(k)
        remote(
            rows_full.at[frm], rows_full.at[frm], gat_ss.at[frm], gat_rs.at[frm], hid=frm
        ).wait_recv()

    loop(1, hids, gather_wait)

    def weight_wait(p):
        def one(k):
            frm = slot_peer(k)
            remote(
                wsend.at[p, frm], wrecv.at[p, frm], w_ss.at[p, frm], w_rs.at[p, frm], slot=frm
            ).wait_recv()

        loop(1, slots, one)

    taken = slots * cap
    mixed = None
    for h in range(hids):
        p, inner = divmod(h * quarter, half)
        if inner == 0:
            weight_wait(p)
        mat = wrecv[p, :, :, inner : inner + quarter].reshape(slots * pair, quarter)
        term = lax.dot_general(
            mat, rows_full[h].reshape(taken, quarter), ACROSS, preferred_element_type=F32
        )
        mixed = term if mixed is None else mixed + term
    mixed = mixed.reshape(slots, pair, taken)
    gate = mixed[:, :owned]
    hidden = gate * jax.nn.sigmoid(gate) * mixed[:, owned:]
    blank = jnp.zeros_like(hidden)
    low_hid = jnp.concatenate([hidden, blank], axis=1).reshape(slots * pair, taken)
    high_hid = jnp.concatenate([blank, hidden], axis=1).reshape(slots * pair, taken)
    low_hid = jnp.transpose(low_hid).astype(BF16)
    high_hid = jnp.transpose(high_hid).astype(BF16)
    weight_wait(2)
    for b in range(hids):
        side, inner = divmod(b * quarter, half)
        mat = wrecv[2, :, :, inner : inner + quarter].reshape(slots * pair, quarter)
        got = jnp.dot(low_hid if side == 0 else high_hid, mat, preferred_element_type=F32)
        out_part[b] = got.astype(BF16).reshape(slots, cap, quarter)

    pos = lax.rem(me_h, 2)
    grp = me_h // 2
    mate = grp * 2 + 1 - pos
    far = (1 - grp) * 2 + pos

    def lev1_copy(g):
        return remote(
            out_part.at[2 * g + 1 - pos], lev1.at[g], l1_ss.at[g], l1_rs.at[g], hid=mate
        )

    lev1_copy(1 - grp).start()
    lev1_copy(grp).start()
    lev1_copy(1 - grp).wait_recv()

    def lev2_copy(s):
        return remote(lev2_send.at[s], lev2.at[s], l2_ss.at[s], l2_rs.at[s], hid=far)

    def to_far(k):
        s = slot_peer(k)
        both = out_part[far, s].astype(F32) + lev1[1 - grp, s].astype(F32)
        lev2_send[s] = both.astype(BF16)
        lev2_copy(s).start()

    loop(1, slots + 1, to_far)
    lev1_copy(grp).wait_recv()

    def ret_copy(to):
        return remote(
            ret_send.at[to], ret_recv.at[me_s], ret_ss.at[to], ret_rs.at[me_s], slot=to
        )

    def last_sum(s):
        lev2_copy(s).wait_recv()
        own = out_part[me_h, s].astype(F32) + lev1[grp, s].astype(F32)
        return (own + lev2[s].astype(F32)).astype(BF16)

    def give_back(k):
        s = slot_peer(k)
        ret_send[s] = last_sum(s)
        ret_copy(s).start()

    loop(1, slots, give_back)
    ret_recv[me_s] = last_sum(me_s)

    def ret_wait(k):
        frm = slot_peer(k)
        remote(
            ret_send.at[frm], ret_recv.at[frm], ret_ss.at[frm], ret_rs.at[frm], slot=frm
        ).wait_recv()

    loop(1, slots, ret_wait)
    out_ref[...] = jnp.dot(
        back_map[...], ret_recv[...].reshape(taken, quarter), preferred_element_type=F32
    ).astype(BF16)

    def slot_sends(k):
        to = slot_peer(k)
        row_copy(to).wait_send()
        tot_copy(to).wait_send()
        for p in range(3):
            grad_copy(p, to).wait_send()
            weight_copy(p, to).wait_send()
        ret_copy(to).wait_send()

    def hid_sends(k):
        to = hid_peer(k)
        part_copy(to).wait_send()
        gather_copy(to).wait_send()

    loop(1, slots, slot_sends)
    loop(1, hids, hid_sends)
    loop(0, slots, lambda s: lev2_copy(s).wait_send())
    for g in range(2):
        lev1_copy(g).wait_send()
    for i, (_, dst, new) in enumerate(state):
        pltpu.make_async_copy(dst, new, store_sem.at[i]).wait()


def fused_shards(
    master,
    first_moment,
    second_moment,
    slot_weights,
    back_rows,
    readout,
    ref_logratio,
    labels,
    place_cur,
    place_next,
    fwd_rows,
    routes,
):
    slots = lax.axis_size("slot")
    hids = lax.axis_size("hid")
    experts = master.shape[0]
    _, kinds, units, width = slot_weights.shape
    owned = units // slots
    rows = back_rows.shape[1]
    half = width // 2
    quarter = fwd_rows.shape[1]
    cap = 2 * fwd_rows.shape[0] // slots
    taken = slots * cap
    target = routes[:, 0]
    target_map = (target[:, None] == jnp.arange(slots, dtype=jnp.int32)[None, :]).astype(jnp.int32)
    earlier = jnp.cumsum(target_map, axis=0) - target_map
    position = jnp.sum(earlier * target_map, axis=1)
    slot_place = target * cap + position
    back_map = (slot_place[:, None] == jnp.arange(taken, dtype=jnp.int32)[None, :]).astype(BF16)
    buffer_rows = lax.dot_general(
        back_map, fwd_rows, (((0,), (0,)), ((), ())), preferred_element_type=F32
    ).astype(BF16)
    sign = jnp.where(labels == 1, -desired_weight, undesired_weight).astype(F32)
    lines = (experts * kinds, owned * width // 128, 128)
    vmem = pl.BlockSpec(memory_space=pltpu.VMEM)
    smem = pl.BlockSpec(memory_space=pltpu.SMEM)
    anywhere = pl.BlockSpec(memory_space=pl.ANY)
    pieces = (3, slots, 2 * owned, half)
    dma = pltpu.SemaphoreType.DMA
    scratch = [
        pltpu.VMEM((kinds, units, width), BF16),
        pltpu.VMEM((rows, width), BF16),
        pltpu.VMEM((rows, width), BF16),
        pltpu.VMEM(lines, F32),
        pltpu.VMEM(lines, F32),
        pltpu.VMEM(lines, F32),
        pltpu.VMEM((units, rows), F32),
        pltpu.VMEM((units, rows), F32),
        pltpu.VMEM((units, rows), F32),
        pltpu.VMEM((2 * units, rows), BF16),
        pltpu.VMEM((units, rows), BF16),
        pltpu.VMEM(pieces, BF16),
        pltpu.VMEM(pieces, BF16),
        pltpu.VMEM(pieces, BF16),
        pltpu.VMEM(pieces, BF16),
        pltpu.VMEM((hids, slots, cap, quarter), BF16),
        pltpu.VMEM((1, rows), F32),
        pltpu.VMEM((hids, 1, rows), F32),
        pltpu.VMEM((1, 128), F32),
        pltpu.VMEM((slots, 1, 128), F32),
        pltpu.VMEM((hids, slots, cap, quarter), BF16),
        pltpu.VMEM((2, slots, cap, quarter), BF16),
        pltpu.VMEM((slots, cap, quarter), BF16),
        pltpu.VMEM((slots, cap, quarter), BF16),
        pltpu.VMEM((slots, cap, quarter), BF16),
        pltpu.VMEM((slots, cap, quarter), BF16),
        dma((1,)),
        dma((2, rows // ROW_STEP)),
        dma((3,)),
        dma((3,)),
        dma((slots,)),
        dma((slots,)),
        dma((hids,)),
        dma((hids,)),
        dma((hids,)),
        dma((hids,)),
        dma((slots,)),
        dma((slots,)),
        dma((3, slots)),
        dma((3, slots)),
        dma((3, slots)),
        dma((3, slots)),
        dma((2,)),
        dma((2,)),
        dma((slots,)),
        dma((slots,)),
        dma((slots,)),
        dma((slots,)),
    ]
    state_shape = jax.ShapeDtypeStruct(lines, F32)
    out_rows, new_master, new_first, new_second = pl.pallas_call(
        functools.partial(kto_kernel, slots, hids, owned, experts),
        out_shape=(
            jax.ShapeDtypeStruct(fwd_rows.shape, BF16),
            state_shape,
            state_shape,
            state_shape,
        ),
        in_specs=[smem, smem, vmem, vmem, vmem, vmem] + [anywhere] * 6,
        out_specs=(vmem, anywhere, anywhere, anywhere),
        scratch_shapes=scratch,
        compiler_params=pltpu.CompilerParams(
            collective_id=0, has_side_effects=True, vmem_limit_bytes=VMEM_BYTES
        ),
        cost_estimate=pl.CostEstimate(
            flops=2 * (6 * rows + 3 * taken) * units * width,
            bytes_accessed=24 * master.size + 4 * rows * width,
            transcendentals=2 * rows * units,
        ),
    )(
        place_cur,
        place_next,
        buffer_rows.reshape(slots, cap, quarter),
        back_map,
        ref_logratio,
        sign,
        slot_weights[0],
        back_rows[0],
        readout[0],
        master.reshape(lines),
        first_moment.reshape(lines),
        second_moment.reshape(lines),
    )
    shape = master.shape
    return (out_rows, new_master.reshape(shape), new_first.reshape(shape), new_second.reshape(shape))


VMEM_BYTES = 60 * 1024 * 1024


def step(*arrays):
    slots = lax.axis_size("slot")
    weights, fwd_rows = arrays[3], arrays[10]
    owned = weights.shape[2] // slots
    cap = 2 * fwd_rows.shape[0] // slots
    fits = owned % 8 == 0 and cap % 16 == 0 and lax.axis_size("hid") == 4
    fits = fits and weights.shape[3] == 4 * fwd_rows.shape[1] and weights.shape[3] % 1024 == 0
    fits = fits and arrays[4].shape[1] % ROW_STEP == 0
    return (fused_shards if fits else shards)(*arrays)


def solution(mesh):
    return jax.shard_map(
        step,
        mesh=mesh,
        in_specs=(
            P(None, None, "hid", "slot"),
            P(None, None, "hid", "slot"),
            P(None, None, "hid", "slot"),
            P("slot", None, "hid", None),
            P("slot", None, None),
            P("slot", None, None),
            P("slot", None),
            P("slot", None),
            P(),
            P(),
            P("slot", "hid"),
            P("slot", None),
        ),
        out_specs=(
            P("slot", "hid"),
            P(None, None, "hid", "slot"),
            P(None, None, "hid", "slot"),
            P(None, None, "hid", "slot"),
        ),
        check_vma=False,
    )
```

```python
import functools

import jax
import jax.numpy as jnp
from jax import lax
from jax.experimental import pallas as pl
from jax.experimental.pallas import tpu as pltpu
from jax.sharding import PartitionSpec as P

beta_kto = 1.0
desired_weight = 1.0
undesired_weight = 1.33
learn_rate = 0.004
decay_first = 0.9
decay_second = 0.999
correct_first = 0.9999734386011124
correct_second = 0.09520785288629043
adam_eps = 1e-08
weight_decay = 0.1


def expert_pass(inputs, weights):
    across = (((1,), (1,)), ((), ()))
    gate_vals = lax.dot_general(inputs, weights[0], across, preferred_element_type=jnp.float32)
    up_vals = lax.dot_general(inputs, weights[1], across, preferred_element_type=jnp.float32)
    hidden = (gate_vals * jax.nn.sigmoid(gate_vals) * up_vals).astype(jnp.bfloat16)
    produced = jnp.dot(hidden, weights[2], preferred_element_type=jnp.float32)
    return (gate_vals, up_vals, hidden, produced)


def kto_slope(scores, labels, center):
    sigma_v = jax.nn.sigmoid(beta_kto * (scores - center))
    signed = jnp.where(labels == 1, -desired_weight, undesired_weight)
    return beta_kto * sigma_v * (1.0 - sigma_v) * signed


def expert_backward(inputs, direction, weights, slope, gate_vals, up_vals, hidden):
    d_expert = (slope[:, None] * direction.astype(jnp.float32)).astype(jnp.bfloat16)
    d_hidden = lax.dot_general(
        d_expert, weights[2], (((1,), (1,)), ((), ())), preferred_element_type=jnp.float32
    )
    sigma_g = jax.nn.sigmoid(gate_vals)
    d_gate = (d_hidden * up_vals * sigma_g * (1.0 + gate_vals * (1.0 - sigma_g))).astype(
        jnp.bfloat16
    )
    d_up = (d_hidden * gate_vals * sigma_g).astype(jnp.bfloat16)
    contract = (((0,), (0,)), ((), ()))
    grad_gate = lax.dot_general(d_gate, inputs, contract, preferred_element_type=jnp.float32)
    grad_up = lax.dot_general(d_up, inputs, contract, preferred_element_type=jnp.float32)
    grad_down = lax.dot_general(hidden, d_expert, contract, preferred_element_type=jnp.float32)
    return jnp.stack([grad_gate, grad_up, grad_down])


def adamw_update(master, first_moment, second_moment, summed):
    new_first = decay_first * first_moment + (1.0 - decay_first) * summed
    new_second = decay_second * second_moment + (1.0 - decay_second) * summed * summed
    update = new_first / correct_first / (jnp.sqrt(new_second / correct_second) + adam_eps)
    new_master = master - learn_rate * (update + weight_decay * master)
    return (new_master, new_first, new_second)


def shards(
    master,
    first_moment,
    second_moment,
    slot_weights,
    back_rows,
    readout,
    ref_logratio,
    labels,
    place_cur,
    place_next,
    fwd_rows,
    routes,
):
    slot_count = lax.axis_size("slot")
    experts_here = master.shape[0]
    weights = slot_weights[0]
    width = weights.shape[2]
    owned_units = master.shape[3] // width
    inputs = back_rows[0]
    direction = readout[0]
    gate_vals, up_vals, hidden, partial_value = expert_pass(inputs, weights)
    row_part = jnp.sum(partial_value * direction.astype(jnp.float32), axis=1)
    policy = lax.psum(row_part, "hid")
    scores = policy - ref_logratio[0]
    row_total = slot_count * inputs.shape[0]
    center = lax.psum(jnp.sum(scores), "slot") / row_total
    slope = kto_slope(scores, labels[0], center)
    grads = expert_backward(inputs, direction, weights, slope, gate_vals, up_vals, hidden)
    arrived = lax.all_to_all(
        grads[None].astype(jnp.bfloat16), "slot", split_axis=2, concat_axis=0, tiled=True
    ).astype(jnp.float32)
    arrived = arrived.reshape(slot_count, 3, 1, owned_units * width)
    owner_map = (place_cur[None, :] == jnp.arange(experts_here, dtype=jnp.int32)[:, None]).astype(
        jnp.float32
    )
    summed = jnp.einsum("es,sabc->eabc", owner_map, arrived, precision=lax.Precision.HIGHEST)
    new_master, new_first, new_second = adamw_update(master, first_moment, second_moment, summed)
    refreshed = new_master.astype(jnp.bfloat16)
    pick_map = (place_next[:, None] == jnp.arange(experts_here, dtype=jnp.int32)[None, :]).astype(
        jnp.bfloat16
    )
    picked = jnp.einsum(
        "se,eabc->sabc", pick_map, refreshed, preferred_element_type=jnp.float32
    ).astype(jnp.bfloat16)
    picked = picked.reshape(slot_count, 3, owned_units, width)
    resident = lax.all_to_all(picked, "slot", split_axis=0, concat_axis=2, tiled=True)[0]
    capacity = 2 * fwd_rows.shape[0] // slot_count
    quarter = fwd_rows.shape[1]
    target = routes[:, 0]
    target_map = (target[:, None] == jnp.arange(slot_count, dtype=jnp.int32)[None, :]).astype(
        jnp.int32
    )
    earlier = jnp.cumsum(target_map, axis=0) - target_map
    position = jnp.sum(earlier * target_map, axis=1)
    slot_place = target * capacity + position
    place_map = (
        slot_place[None, :] == jnp.arange(slot_count * capacity, dtype=jnp.int32)[:, None]
    ).astype(jnp.bfloat16)
    buffer_rows = jnp.dot(place_map, fwd_rows, preferred_element_type=jnp.float32).astype(
        jnp.bfloat16
    )
    buffer_rows = buffer_rows.reshape(slot_count, capacity, quarter)
    arrived_rows = lax.all_to_all(
        buffer_rows, "slot", split_axis=0, concat_axis=0, tiled=True
    ).reshape(slot_count * capacity, quarter)
    across = (((1,), (1,)), ((), ()))
    piece_rows = lax.all_gather(arrived_rows, "hid", axis=1, tiled=True)
    gate_cols = resident[0]
    up_cols = resident[1]
    fwd_gate = lax.dot_general(piece_rows, gate_cols, across, preferred_element_type=jnp.float32)
    fwd_up = lax.dot_general(piece_rows, up_cols, across, preferred_element_type=jnp.float32)
    fwd_hidden = (fwd_gate * jax.nn.sigmoid(fwd_gate) * fwd_up).astype(jnp.bfloat16)
    fwd_partial = jnp.dot(fwd_hidden, resident[2], preferred_element_type=jnp.float32)
    totals = lax.psum(fwd_partial, "hid")
    shares = lax.dynamic_slice_in_dim(totals, lax.axis_index("hid") * quarter, quarter, 1)
    outgoing = shares.astype(jnp.bfloat16).reshape(slot_count, capacity, quarter)
    returned = lax.all_to_all(outgoing, "slot", split_axis=0, concat_axis=0, tiled=True).reshape(
        slot_count * capacity, quarter
    )
    out_rows = lax.dot_general(
        place_map, returned, (((0,), (0,)), ((), ())), preferred_element_type=jnp.float32
    ).astype(jnp.bfloat16)
    return (out_rows, new_master, new_first, new_second)


ACROSS = (((1,), (1,)), ((), ()))
F32 = jnp.float32
BF16 = jnp.bfloat16
MESH = pl.DeviceIdType.MESH
ROW_STEP = 256


def kto_kernel(
    slots,
    hids,
    owned,
    experts,
    place_cur,
    place_next,
    route_ref,
    label_ref,
    ref_ref,
    fwd_hbm,
    w_hbm,
    x_hbm,
    r_hbm,
    mast_hbm,
    mom1_hbm,
    mom2_hbm,
    out_ref,
    nmast_hbm,
    nmom1_hbm,
    nmom2_hbm,
    fwd_v,
    rows_in,
    back_map,
    w_v,
    x_v,
    r_v,
    mast_v,
    mom1_v,
    mom2_v,
    pre_gate,
    pre_up,
    hid_v,
    d_gu,
    d_hid,
    gsend,
    grecv,
    wsend,
    wrecv,
    rows_full,
    part_v,
    part_all,
    tot_v,
    tot_all,
    side_hid,
    out_part,
    lev1,
    lev2_send,
    lev2,
    ret_send,
    ret_recv,
    load_sem,
    xr_sem,
    mom_sem,
    store_sem,
    row_ss,
    row_rs,
    gat_ss,
    gat_rs,
    part_ss,
    part_rs,
    tot_ss,
    tot_rs,
    g_ss,
    g_rs,
    w_ss,
    w_rs,
    l1_ss,
    l1_rs,
    l2_ss,
    l2_rs,
    ret_ss,
    ret_rs,
):
    me_s = lax.axis_index("slot")
    me_h = lax.axis_index("hid")
    width = w_v.shape[2]
    half = width // 2
    quarter = rows_in.shape[2]
    cap = rows_in.shape[1]
    taken = slots * cap
    pair = 2 * owned
    rows = x_v.shape[0]
    mixing = width // quarter
    pieces = mixing + half // quarter
    steps = rows // ROW_STEP

    def slot_peer(k):
        return lax.rem(me_s + k, slots)

    def hid_peer(k):
        return lax.rem(me_h + k, hids)

    def remote(src, dst, ssem, rsem, slot=None, hid=None):
        return pltpu.make_async_remote_copy(
            src_ref=src,
            dst_ref=dst,
            send_sem=ssem,
            recv_sem=rsem,
            device_id=(me_s if slot is None else slot, me_h if hid is None else hid),
            device_id_type=MESH,
        )

    def loop(low, high, body):
        def step(i, carry):
            body(i)
            return carry

        lax.fori_loop(low, high, step, 0)

    fwd_load = pltpu.make_async_copy(fwd_hbm, fwd_v, load_sem.at[1])
    fwd_load.start()
    w_load = pltpu.make_async_copy(w_hbm, w_v, load_sem.at[0])
    w_load.start()

    def xr_copies(c):
        at = pl.ds(pl.multiple_of(c * ROW_STEP, ROW_STEP), ROW_STEP)
        return (
            pltpu.make_async_copy(x_hbm.at[at], x_v.at[at], xr_sem.at[0, c]),
            pltpu.make_async_copy(r_hbm.at[at], r_v.at[at], xr_sem.at[1, c]),
        )

    def start_xr(c):
        for copy in xr_copies(c):
            copy.start()

    loop(0, steps, start_xr)
    state = ((mast_hbm, mast_v, nmast_hbm), (mom1_hbm, mom1_v, nmom1_hbm), (mom2_hbm, mom2_v, nmom2_hbm))
    for i, (src, dst, _) in enumerate(state):
        pltpu.make_async_copy(src, dst, mom_sem.at[i]).start()

    barrier = pltpu.get_barrier_semaphore()

    def greet_slot(k):
        pl.semaphore_signal(barrier, inc=1, device_id=(slot_peer(k), me_h), device_id_type=MESH)

    def greet_hid(k):
        pl.semaphore_signal(barrier, inc=1, device_id=(me_s, hid_peer(k)), device_id_type=MESH)

    loop(1, slots, greet_slot)
    loop(1, hids, greet_hid)

    count = fwd_v.shape[0]
    named = jnp.broadcast_to(route_ref[...].astype(F32), (count, count))
    first = lax.broadcasted_iota(jnp.int32, (count, count), 0)
    second = lax.broadcasted_iota(jnp.int32, (count, count), 1)
    before = (named == jnp.transpose(named)) & (first < second)
    rank = jnp.sum(jnp.where(before, 1.0, 0.0), axis=0, keepdims=True)
    place = named[:1] * cap + rank
    spot = lax.broadcasted_iota(jnp.int32, (taken, count), 0).astype(F32)
    place_map = jnp.where(spot == place, 1.0, 0.0)
    back_map[...] = jnp.transpose(place_map).astype(BF16)
    fwd_load.wait()
    rows_in[...] = (
        jnp.dot(place_map.astype(BF16), fwd_v[...], preferred_element_type=F32)
        .astype(BF16)
        .reshape(slots, cap, quarter)
    )
    pl.semaphore_wait(barrier, slots + hids - 2)

    def row_copy(to):
        return remote(
            rows_in.at[to], rows_full.at[me_h, me_s], row_ss.at[to], row_rs.at[me_s], slot=to
        )

    loop(1, slots, lambda k: row_copy(slot_peer(k)).start())
    rows_full[me_h, me_s] = rows_in[me_s]

    w_load.wait()

    def first_half(c):
        for copy in xr_copies(c):
            copy.wait()
        at = pl.ds(pl.multiple_of(c * ROW_STEP, ROW_STEP), ROW_STEP)
        xc = x_v[at, :]
        rc = r_v[at, :]
        gate = lax.dot_general(w_v[0], xc, ACROSS, preferred_element_type=F32)
        up = lax.dot_general(w_v[1], xc, ACROSS, preferred_element_type=F32)
        turn = lax.dot_general(w_v[2], rc, ACROSS, preferred_element_type=F32)
        sig = jax.nn.sigmoid(gate)
        act = gate * sig
        hidden = (act * up).astype(BF16).astype(F32)
        part_v[:, at] = jnp.sum(hidden * turn, axis=0, keepdims=True)
        pre_gate[:, at] = turn * up * sig * (1.0 + gate * (1.0 - sig))
        pre_up[:, at] = turn * act
        hid_v[:, at] = hidden

    loop(0, steps, first_half)

    def part_copy(to):
        return remote(part_v, part_all.at[me_h], part_ss.at[to], part_rs.at[me_h], hid=to)

    loop(1, hids, lambda k: part_copy(hid_peer(k)).start())
    part_all[me_h] = part_v[...]

    def part_wait(k):
        frm = hid_peer(k)
        remote(part_v, part_all.at[frm], part_ss.at[frm], part_rs.at[frm], hid=frm).wait_recv()

    loop(1, hids, part_wait)
    policy = part_all[0]
    for h in range(1, hids):
        policy = policy + part_all[h]
    scores = policy - ref_ref[...]
    tot_v[...] = jnp.broadcast_to(jnp.sum(scores, axis=1, keepdims=True), tot_v.shape)

    def tot_copy(to):
        return remote(tot_v, tot_all.at[me_s], tot_ss.at[to], tot_rs.at[me_s], slot=to)

    loop(1, slots, lambda k: tot_copy(slot_peer(k)).start())
    tot_all[me_s] = tot_v[...]

    def tot_wait(k):
        frm = slot_peer(k)
        remote(tot_v, tot_all.at[frm], tot_ss.at[frm], tot_rs.at[frm], slot=frm).wait_recv()

    loop(1, slots, tot_wait)
    total = tot_all[0]
    for s in range(1, slots):
        total = total + tot_all[s]
    center = total[:, :1] * (1.0 / (slots * rows))
    slope = kto_slope(scores, label_ref[...], center)

    for s in range(slots):
        units = pl.ds(s * owned, owned)
        both = jnp.concatenate([pre_gate[units, :] * slope, pre_up[units, :] * slope], axis=0)
        d_gu[pl.ds(s * pair, pair), :] = both.astype(BF16)
    d_hid[...] = (hid_v[...] * slope).astype(BF16)

    def grad_copy(p, to):
        return remote(
            gsend.at[p, to], grecv.at[p, me_s], g_ss.at[p, to], g_rs.at[p, me_s], slot=to
        )

    def send_grads(p):
        loop(1, slots, lambda k: grad_copy(p, slot_peer(k)).start())
        grecv[p, me_s] = gsend[p, me_s]

    def mixing_grads(p):
        at = pl.ds(pl.multiple_of(p * quarter, quarter), quarter)
        found = jnp.dot(d_gu[...], x_v[:, at], preferred_element_type=F32)
        gsend[p] = found.astype(BF16).reshape(slots, pair, quarter)
        send_grads(p)

    def down_grads(p):
        low = pl.ds(pl.multiple_of((p - mixing) * quarter, quarter), quarter)
        high = pl.ds(pl.multiple_of(half + (p - mixing) * quarter, quarter), quarter)
        low_part = jnp.dot(d_hid[...], r_v[:, low], preferred_element_type=F32)
        high_part = jnp.dot(d_hid[...], r_v[:, high], preferred_element_type=F32)
        both = jnp.concatenate(
            [low_part.reshape(slots, owned, quarter), high_part.reshape(slots, owned, quarter)],
            axis=1,
        )
        gsend[p] = both.astype(BF16)
        send_grads(p)

    loop(0, mixing, mixing_grads)
    loop(mixing, pieces, down_grads)

    def row_wait(k):
        frm = slot_peer(k)
        remote(
            rows_in.at[frm], rows_full.at[me_h, frm], row_ss.at[frm], row_rs.at[frm], slot=frm
        ).wait_recv()

    loop(1, slots, row_wait)

    def gather_copy(to):
        return remote(
            rows_full.at[me_h], rows_full.at[me_h], gat_ss.at[to], gat_rs.at[me_h], hid=to
        )

    loop(1, hids, lambda k: gather_copy(hid_peer(k)).start())

    for i, (src, dst, _) in enumerate(state):
        pltpu.make_async_copy(src, dst, mom_sem.at[i]).wait()
    cur = [place_cur[s] for s in range(slots)]
    nxt = [place_next[s] for s in range(slots)]
    is_cur = [[jnp.where(cur[s] == e, 1.0, 0.0) for s in range(slots)] for e in range(experts)]
    is_nxt = [[jnp.where(nxt[t] == e, 1.0, 0.0) for t in range(slots)] for e in range(experts)]
    blocks = width // 128
    part_blocks = quarter // 128

    def weight_copy(p, to):
        return remote(
            wsend.at[p, to], wrecv.at[p, me_s], w_ss.at[p, to], w_rs.at[p, me_s], slot=to
        )

    def adam(p, spots):
        def grad_wait(k):
            frm = slot_peer(k)
            remote(
                gsend.at[p, frm], grecv.at[p, frm], g_ss.at[p, frm], g_rs.at[p, frm], slot=frm
            ).wait_recv()

        loop(1, slots, grad_wait)

        def lane_block(j):
            lanes = pl.ds(pl.multiple_of(j * 128, 128), 128)
            came = [grecv[p, s, :, lanes].astype(F32) for s in range(slots)]
            fresh = []
            for e in range(experts):
                summed = came[0] * is_cur[e][0]
                for s in range(1, slots):
                    summed = summed + came[s] * is_cur[e][s]
                sides = []
                for side, (kind, block) in enumerate(spots(j)):
                    row = e * 3 + kind
                    at = pl.ds(block, owned, stride=blocks)
                    new_m, new_1, new_2 = adamw_update(
                        mast_v[row, at, :],
                        mom1_v[row, at, :],
                        mom2_v[row, at, :],
                        summed[side * owned : (side + 1) * owned],
                    )
                    mast_v[row, at, :] = new_m
                    mom1_v[row, at, :] = new_1
                    mom2_v[row, at, :] = new_2
                    sides.append(new_m)
                fresh.append(jnp.concatenate(sides, axis=0))
            for t in range(slots):
                chosen = fresh[0] * is_nxt[0][t]
                for e in range(1, experts):
                    chosen = chosen + fresh[e] * is_nxt[e][t]
                wsend[p, t, :, lanes] = chosen.astype(BF16)

        loop(0, part_blocks, lane_block)
        loop(1, slots, lambda k: weight_copy(p, slot_peer(k)).start())
        wrecv[p, me_s] = wsend[p, me_s]

    def mixing_adam(p):
        adam(p, lambda j: [(side, p * part_blocks + j) for side in range(2)])

    def down_adam(p):
        start = (p - mixing) * part_blocks
        adam(p, lambda j: [(2, side * (blocks // 2) + start + j) for side in range(2)])

    loop(0, mixing, mixing_adam)
    loop(mixing, pieces, down_adam)
    for i, (_, dst, new) in enumerate(state):
        pltpu.make_async_copy(dst, new, store_sem.at[i]).start()

    def gather_wait(k):
        frm = hid_peer(k)
        remote(
            rows_full.at[frm], rows_full.at[frm], gat_ss.at[frm], gat_rs.at[frm], hid=frm
        ).wait_recv()

    loop(1, hids, gather_wait)

    def weight_wait(p):
        def one(k):
            frm = slot_peer(k)
            remote(
                wsend.at[p, frm], wrecv.at[p, frm], w_ss.at[p, frm], w_rs.at[p, frm], slot=frm
            ).wait_recv()

        loop(1, slots, one)

    mixed = None
    for h in range(hids):
        weight_wait(h)
        term = lax.dot_general(
            wrecv[h].reshape(slots * pair, quarter),
            rows_full[h].reshape(taken, quarter),
            ACROSS,
            preferred_element_type=F32,
        )
        mixed = term if mixed is None else mixed + term
    mixed = mixed.reshape(slots, pair, taken)
    gate = mixed[:, :owned]
    hidden = gate * jax.nn.sigmoid(gate) * mixed[:, owned:]
    blank = jnp.zeros_like(hidden)
    low_hid = jnp.concatenate([hidden, blank], axis=1).reshape(slots * pair, taken)
    high_hid = jnp.concatenate([blank, hidden], axis=1).reshape(slots * pair, taken)
    side_hid[0] = jnp.transpose(low_hid).astype(BF16)
    side_hid[1] = jnp.transpose(high_hid).astype(BF16)

    pos = lax.rem(me_h, 2)
    grp = me_h // 2
    mate = grp * 2 + 1 - pos
    far = (1 - grp) * 2 + pos

    def lev1_copy(g, turn):
        return remote(out_part.at[2 * g + turn], lev1.at[g], l1_ss.at[g], l1_rs.at[g], hid=mate)

    def lev2_copy(s):
        return remote(lev2_send.at[s], lev2.at[s], l2_ss.at[s], l2_rs.at[s], hid=far)

    def ret_copy(to):
        return remote(
            ret_send.at[to], ret_recv.at[me_s], ret_ss.at[to], ret_rs.at[me_s], slot=to
        )

    def to_far(k):
        s = slot_peer(k)
        both = out_part[far, s].astype(F32) + lev1[1 - grp, s].astype(F32)
        lev2_send[s] = both.astype(BF16)
        lev2_copy(s).start()

    def last_sum(s):
        lev2_copy(s).wait_recv()
        own = out_part[me_h, s].astype(F32) + lev1[grp, s].astype(F32)
        return (own + lev2[s].astype(F32)).astype(BF16)

    def give_back(k):
        s = slot_peer(k)
        ret_send[s] = last_sum(s)
        ret_copy(s).start()

    for turn in range(2):
        weight_wait(mixing + turn)
        for i in range(2):
            g = 1 - grp if i == 0 else grp
            got = jnp.dot(
                side_hid[g],
                wrecv[mixing + turn].reshape(slots * pair, quarter),
                preferred_element_type=F32,
            )
            out_part[2 * g + turn] = got.astype(BF16).reshape(slots, cap, quarter)

            @pl.when(pos != turn)
            def _(g=g, turn=turn):
                lev1_copy(g, turn).start()

        @pl.when(pos == turn)
        def _(turn=turn):
            lev1_copy(1 - grp, turn).wait_recv()
            loop(1, slots + 1, to_far)
            lev1_copy(grp, turn).wait_recv()
            loop(1, slots, give_back)
            ret_recv[me_s] = last_sum(me_s)

    def ret_wait(k):
        frm = slot_peer(k)
        remote(
            ret_send.at[frm], ret_recv.at[frm], ret_ss.at[frm], ret_rs.at[frm], slot=frm
        ).wait_recv()

    loop(1, slots, ret_wait)
    out_ref[...] = jnp.dot(
        back_map[...], ret_recv[...].reshape(taken, quarter), preferred_element_type=F32
    ).astype(BF16)

    def slot_sends(k):
        to = slot_peer(k)
        row_copy(to).wait_send()
        tot_copy(to).wait_send()
        for p in range(pieces):
            grad_copy(p, to).wait_send()
            weight_copy(p, to).wait_send()
        ret_copy(to).wait_send()

    def hid_sends(k):
        to = hid_peer(k)
        part_copy(to).wait_send()
        gather_copy(to).wait_send()

    loop(1, slots, slot_sends)
    loop(1, hids, hid_sends)
    loop(0, slots, lambda s: lev2_copy(s).wait_send())
    for g in range(2):
        lev1_copy(g, 1 - pos).wait_send()
    for i, (_, dst, new) in enumerate(state):
        pltpu.make_async_copy(dst, new, store_sem.at[i]).wait()


def results_kernel(rows_ref, mast_in, mom1_in, mom2_in, out_ref, mast_out, mom1_out, mom2_out, held, sem):
    parts = sem.shape[2]
    size = held.shape[1] // parts

    src = (mast_in, mom1_in, mom2_in)
    dst = (mast_out, mom1_out, mom2_out)

    def come(i, c):
        at = pl.ds(c * size, size)
        return pltpu.make_async_copy(src[i].at[at], held.at[i, at], sem.at[0, i, c])

    def go(i, c):
        at = pl.ds(c * size, size)
        return pltpu.make_async_copy(held.at[i, at], dst[i].at[at], sem.at[1, i, c])

    every = [(i, c) for i in range(3) for c in range(parts)]
    for i, c in every:
        come(i, c).start()
    out_ref[...] = rows_ref[...]
    for i, c in every:
        come(i, c).wait()
        go(i, c).start()
    for i, c in every:
        go(i, c).wait()


def fused_shards(
    master,
    first_moment,
    second_moment,
    slot_weights,
    back_rows,
    readout,
    ref_logratio,
    labels,
    place_cur,
    place_next,
    fwd_rows,
    routes,
):
    slots = lax.axis_size("slot")
    hids = lax.axis_size("hid")
    experts = master.shape[0]
    _, kinds, units, width = slot_weights.shape
    owned = units // slots
    rows = back_rows.shape[1]
    half = width // 2
    quarter = fwd_rows.shape[1]
    cap = 2 * fwd_rows.shape[0] // slots
    taken = slots * cap
    lines = (experts * kinds, owned * width // 128, 128)
    vmem = pl.BlockSpec(memory_space=pltpu.VMEM)
    smem = pl.BlockSpec(memory_space=pltpu.SMEM)
    anywhere = pl.BlockSpec(memory_space=pl.ANY)
    pieces = (width // quarter + half // quarter, slots, 2 * owned, quarter)
    dma = pltpu.SemaphoreType.DMA
    scratch = [
        pltpu.VMEM(fwd_rows.shape, BF16),
        pltpu.VMEM((slots, cap, quarter), BF16),
        pltpu.VMEM((fwd_rows.shape[0], taken), BF16),
        pltpu.VMEM((kinds, units, width), BF16),
        pltpu.VMEM((rows, width), BF16),
        pltpu.VMEM((rows, width), BF16),
        pltpu.VMEM(lines, F32),
        pltpu.VMEM(lines, F32),
        pltpu.VMEM(lines, F32),
        pltpu.VMEM((units, rows), F32),
        pltpu.VMEM((units, rows), F32),
        pltpu.VMEM((units, rows), F32),
        pltpu.VMEM((2 * units, rows), BF16),
        pltpu.VMEM((units, rows), BF16),
        pltpu.VMEM(pieces, BF16),
        pltpu.VMEM(pieces, BF16),
        pltpu.VMEM(pieces, BF16),
        pltpu.VMEM(pieces, BF16),
        pltpu.VMEM((hids, slots, cap, quarter), BF16),
        pltpu.VMEM((1, rows), F32),
        pltpu.VMEM((hids, 1, rows), F32),
        pltpu.VMEM((1, 128), F32),
        pltpu.VMEM((slots, 1, 128), F32),
        pltpu.VMEM((2, taken, 2 * units), BF16),
        pltpu.VMEM((hids, slots, cap, quarter), BF16),
        pltpu.VMEM((2, slots, cap, quarter), BF16),
        pltpu.VMEM((slots, cap, quarter), BF16),
        pltpu.VMEM((slots, cap, quarter), BF16),
        pltpu.VMEM((slots, cap, quarter), BF16),
        pltpu.VMEM((slots, cap, quarter), BF16),
        dma((2,)),
        dma((2, rows // ROW_STEP)),
        dma((3,)),
        dma((3,)),
        dma((slots,)),
        dma((slots,)),
        dma((hids,)),
        dma((hids,)),
        dma((hids,)),
        dma((hids,)),
        dma((slots,)),
        dma((slots,)),
        dma(pieces[:2]),
        dma(pieces[:2]),
        dma(pieces[:2]),
        dma(pieces[:2]),
        dma((2,)),
        dma((2,)),
        dma((slots,)),
        dma((slots,)),
        dma((slots,)),
        dma((slots,)),
    ]
    state_shape = jax.ShapeDtypeStruct(lines, F32)
    out_rows, new_master, new_first, new_second = pl.pallas_call(
        functools.partial(kto_kernel, slots, hids, owned, experts),
        out_shape=(
            jax.ShapeDtypeStruct(fwd_rows.shape, BF16),
            state_shape,
            state_shape,
            state_shape,
        ),
        in_specs=[smem, smem, vmem, vmem, vmem] + [anywhere] * 7,
        out_specs=(vmem, anywhere, anywhere, anywhere),
        scratch_shapes=scratch,
        compiler_params=pltpu.CompilerParams(
            collective_id=0, has_side_effects=True, vmem_limit_bytes=VMEM_BYTES
        ),
        cost_estimate=pl.CostEstimate(
            flops=2 * (6 * rows + 3 * taken) * units * width,
            bytes_accessed=24 * master.size + 4 * rows * width,
            transcendentals=2 * rows * units,
        ),
    )(
        place_cur,
        place_next,
        routes.reshape(1, fwd_rows.shape[0]),
        labels,
        ref_logratio,
        fwd_rows,
        slot_weights[0],
        back_rows[0],
        readout[0],
        master.reshape(lines),
        first_moment.reshape(lines),
        second_moment.reshape(lines),
    )
    out_rows, new_master, new_first, new_second = pl.pallas_call(
        results_kernel,
        out_shape=(
            jax.ShapeDtypeStruct(fwd_rows.shape, BF16),
            state_shape,
            state_shape,
            state_shape,
        ),
        in_specs=[vmem] + [anywhere] * 3,
        out_specs=(vmem, anywhere, anywhere, anywhere),
        scratch_shapes=[pltpu.VMEM((3,) + lines, F32), dma((2, 3, experts))],
        compiler_params=pltpu.CompilerParams(vmem_limit_bytes=VMEM_BYTES),
        cost_estimate=pl.CostEstimate(
            flops=0, bytes_accessed=24 * master.size, transcendentals=0
        ),
    )(out_rows, new_master, new_first, new_second)
    shape = master.shape
    return (out_rows, new_master.reshape(shape), new_first.reshape(shape), new_second.reshape(shape))


VMEM_BYTES = 60 * 1024 * 1024


def step(*arrays):
    slots = lax.axis_size("slot")
    weights, fwd_rows = arrays[3], arrays[10]
    owned = weights.shape[2] // slots
    cap = 2 * fwd_rows.shape[0] // slots
    fits = owned % 8 == 0 and cap % 16 == 0 and lax.axis_size("hid") == 4
    fits = fits and weights.shape[3] == 4 * fwd_rows.shape[1] and weights.shape[3] % 1024 == 0
    fits = fits and arrays[4].shape[1] % ROW_STEP == 0
    return (fused_shards if fits else shards)(*arrays)


def solution(mesh):
    return jax.shard_map(
        step,
        mesh=mesh,
        in_specs=(
            P(None, None, "hid", "slot"),
            P(None, None, "hid", "slot"),
            P(None, None, "hid", "slot"),
            P("slot", None, "hid", None),
            P("slot", None, None),
            P("slot", None, None),
            P("slot", None),
            P("slot", None),
            P(),
            P(),
            P("slot", "hid"),
            P("slot", None),
        ),
        out_specs=(
            P("slot", "hid"),
            P(None, None, "hid", "slot"),
            P(None, None, "hid", "slot"),
            P(None, None, "hid", "slot"),
        ),
        check_vma=False,
    )
```

```python
import functools

import jax
import jax.numpy as jnp
from jax import lax
from jax.experimental import pallas as pl
from jax.experimental.pallas import tpu as pltpu
from jax.sharding import PartitionSpec as P

beta_kto = 1.0
desired_weight = 1.0
undesired_weight = 1.33
learn_rate = 0.004
decay_first = 0.9
decay_second = 0.999
correct_first = 0.9999734386011124
correct_second = 0.09520785288629043
adam_eps = 1e-08
weight_decay = 0.1


def expert_pass(inputs, weights):
    across = (((1,), (1,)), ((), ()))
    gate_vals = lax.dot_general(inputs, weights[0], across, preferred_element_type=jnp.float32)
    up_vals = lax.dot_general(inputs, weights[1], across, preferred_element_type=jnp.float32)
    hidden = (gate_vals * jax.nn.sigmoid(gate_vals) * up_vals).astype(jnp.bfloat16)
    produced = jnp.dot(hidden, weights[2], preferred_element_type=jnp.float32)
    return (gate_vals, up_vals, hidden, produced)


def kto_slope(scores, labels, center):
    sigma_v = jax.nn.sigmoid(beta_kto * (scores - center))
    signed = jnp.where(labels == 1, -desired_weight, undesired_weight)
    return beta_kto * sigma_v * (1.0 - sigma_v) * signed


def expert_backward(inputs, direction, weights, slope, gate_vals, up_vals, hidden):
    d_expert = (slope[:, None] * direction.astype(jnp.float32)).astype(jnp.bfloat16)
    d_hidden = lax.dot_general(
        d_expert, weights[2], (((1,), (1,)), ((), ())), preferred_element_type=jnp.float32
    )
    sigma_g = jax.nn.sigmoid(gate_vals)
    d_gate = (d_hidden * up_vals * sigma_g * (1.0 + gate_vals * (1.0 - sigma_g))).astype(
        jnp.bfloat16
    )
    d_up = (d_hidden * gate_vals * sigma_g).astype(jnp.bfloat16)
    contract = (((0,), (0,)), ((), ()))
    grad_gate = lax.dot_general(d_gate, inputs, contract, preferred_element_type=jnp.float32)
    grad_up = lax.dot_general(d_up, inputs, contract, preferred_element_type=jnp.float32)
    grad_down = lax.dot_general(hidden, d_expert, contract, preferred_element_type=jnp.float32)
    return jnp.stack([grad_gate, grad_up, grad_down])


def adamw_update(master, first_moment, second_moment, summed):
    new_first = decay_first * first_moment + (1.0 - decay_first) * summed
    new_second = decay_second * second_moment + (1.0 - decay_second) * summed * summed
    update = new_first / correct_first / (jnp.sqrt(new_second / correct_second) + adam_eps)
    new_master = master - learn_rate * (update + weight_decay * master)
    return (new_master, new_first, new_second)


def shards(
    master,
    first_moment,
    second_moment,
    slot_weights,
    back_rows,
    readout,
    ref_logratio,
    labels,
    place_cur,
    place_next,
    fwd_rows,
    routes,
):
    slot_count = lax.axis_size("slot")
    experts_here = master.shape[0]
    weights = slot_weights[0]
    width = weights.shape[2]
    owned_units = master.shape[3] // width
    inputs = back_rows[0]
    direction = readout[0]
    gate_vals, up_vals, hidden, partial_value = expert_pass(inputs, weights)
    row_part = jnp.sum(partial_value * direction.astype(jnp.float32), axis=1)
    policy = lax.psum(row_part, "hid")
    scores = policy - ref_logratio[0]
    row_total = slot_count * inputs.shape[0]
    center = lax.psum(jnp.sum(scores), "slot") / row_total
    slope = kto_slope(scores, labels[0], center)
    grads = expert_backward(inputs, direction, weights, slope, gate_vals, up_vals, hidden)
    arrived = lax.all_to_all(
        grads[None].astype(jnp.bfloat16), "slot", split_axis=2, concat_axis=0, tiled=True
    ).astype(jnp.float32)
    arrived = arrived.reshape(slot_count, 3, 1, owned_units * width)
    owner_map = (place_cur[None, :] == jnp.arange(experts_here, dtype=jnp.int32)[:, None]).astype(
        jnp.float32
    )
    summed = jnp.einsum("es,sabc->eabc", owner_map, arrived, precision=lax.Precision.HIGHEST)
    new_master, new_first, new_second = adamw_update(master, first_moment, second_moment, summed)
    refreshed = new_master.astype(jnp.bfloat16)
    pick_map = (place_next[:, None] == jnp.arange(experts_here, dtype=jnp.int32)[None, :]).astype(
        jnp.bfloat16
    )
    picked = jnp.einsum(
        "se,eabc->sabc", pick_map, refreshed, preferred_element_type=jnp.float32
    ).astype(jnp.bfloat16)
    picked = picked.reshape(slot_count, 3, owned_units, width)
    resident = lax.all_to_all(picked, "slot", split_axis=0, concat_axis=2, tiled=True)[0]
    capacity = 2 * fwd_rows.shape[0] // slot_count
    quarter = fwd_rows.shape[1]
    target = routes[:, 0]
    target_map = (target[:, None] == jnp.arange(slot_count, dtype=jnp.int32)[None, :]).astype(
        jnp.int32
    )
    earlier = jnp.cumsum(target_map, axis=0) - target_map
    position = jnp.sum(earlier * target_map, axis=1)
    slot_place = target * capacity + position
    place_map = (
        slot_place[None, :] == jnp.arange(slot_count * capacity, dtype=jnp.int32)[:, None]
    ).astype(jnp.bfloat16)
    buffer_rows = jnp.dot(place_map, fwd_rows, preferred_element_type=jnp.float32).astype(
        jnp.bfloat16
    )
    buffer_rows = buffer_rows.reshape(slot_count, capacity, quarter)
    arrived_rows = lax.all_to_all(
        buffer_rows, "slot", split_axis=0, concat_axis=0, tiled=True
    ).reshape(slot_count * capacity, quarter)
    across = (((1,), (1,)), ((), ()))
    piece_rows = lax.all_gather(arrived_rows, "hid", axis=1, tiled=True)
    gate_cols = resident[0]
    up_cols = resident[1]
    fwd_gate = lax.dot_general(piece_rows, gate_cols, across, preferred_element_type=jnp.float32)
    fwd_up = lax.dot_general(piece_rows, up_cols, across, preferred_element_type=jnp.float32)
    fwd_hidden = (fwd_gate * jax.nn.sigmoid(fwd_gate) * fwd_up).astype(jnp.bfloat16)
    fwd_partial = jnp.dot(fwd_hidden, resident[2], preferred_element_type=jnp.float32)
    totals = lax.psum(fwd_partial, "hid")
    shares = lax.dynamic_slice_in_dim(totals, lax.axis_index("hid") * quarter, quarter, 1)
    outgoing = shares.astype(jnp.bfloat16).reshape(slot_count, capacity, quarter)
    returned = lax.all_to_all(outgoing, "slot", split_axis=0, concat_axis=0, tiled=True).reshape(
        slot_count * capacity, quarter
    )
    out_rows = lax.dot_general(
        place_map, returned, (((0,), (0,)), ((), ())), preferred_element_type=jnp.float32
    ).astype(jnp.bfloat16)
    return (out_rows, new_master, new_first, new_second)


ACROSS = (((1,), (1,)), ((), ()))
F32 = jnp.float32
BF16 = jnp.bfloat16
MESH = pl.DeviceIdType.MESH
ROW_STEP = 256


def kto_kernel(
    slots,
    hids,
    owned,
    experts,
    place_cur,
    place_next,
    route_ref,
    label_ref,
    ref_ref,
    fwd_hbm,
    w_hbm,
    x_hbm,
    r_hbm,
    mast_hbm,
    mom1_hbm,
    mom2_hbm,
    out_hbm,
    nmast_hbm,
    nmom1_hbm,
    nmom2_hbm,
    fwd_v,
    rows_in,
    back_map,
    w_v,
    x_v,
    r_v,
    mast_v,
    mom1_v,
    mom2_v,
    pre_gate,
    pre_up,
    hid_v,
    d_gu,
    d_hid,
    gsend,
    grecv,
    wsend,
    wrecv,
    rows_full,
    part_v,
    part_all,
    tot_v,
    tot_all,
    side_hid,
    out_part,
    lev1,
    lev2_send,
    lev2,
    ret_send,
    ret_recv,
    load_sem,
    xr_sem,
    mom_sem,
    store_sem,
    row_ss,
    row_rs,
    gat_ss,
    gat_rs,
    part_ss,
    part_rs,
    tot_ss,
    tot_rs,
    g_ss,
    g_rs,
    w_ss,
    w_rs,
    l1_ss,
    l1_rs,
    l2_ss,
    l2_rs,
    ret_ss,
    ret_rs,
):
    me_s = lax.axis_index("slot")
    me_h = lax.axis_index("hid")
    units, width = w_v.shape[1:]
    half = width // 2
    quarter = rows_in.shape[2]
    cap = rows_in.shape[1]
    taken = slots * cap
    pair = 2 * owned
    rows = x_v.shape[0]
    mixing = width // quarter
    pieces = mixing + half // quarter
    steps = rows // ROW_STEP

    def slot_peer(k):
        return lax.rem(me_s + k, slots)

    def hid_peer(k):
        return lax.rem(me_h + k, hids)

    def remote(src, dst, ssem, rsem, slot=None, hid=None):
        return pltpu.make_async_remote_copy(
            src_ref=src,
            dst_ref=dst,
            send_sem=ssem,
            recv_sem=rsem,
            device_id=(me_s if slot is None else slot, me_h if hid is None else hid),
            device_id_type=MESH,
        )

    def loop(low, high, body):
        def step(i, carry):
            body(i)
            return carry

        lax.fori_loop(low, high, step, 0)

    fwd_load = pltpu.make_async_copy(fwd_hbm, fwd_v, load_sem.at[1])
    fwd_load.start()
    w_load = pltpu.make_async_copy(w_hbm, w_v, load_sem.at[0])
    w_load.start()

    def xr_copies(c):
        at = pl.ds(pl.multiple_of(c * ROW_STEP, ROW_STEP), ROW_STEP)
        return (
            pltpu.make_async_copy(x_hbm.at[at], x_v.at[at], xr_sem.at[0, c]),
            pltpu.make_async_copy(r_hbm.at[at], r_v.at[at], xr_sem.at[1, c]),
        )

    def start_xr(c):
        for copy in xr_copies(c):
            copy.start()

    loop(0, steps, start_xr)
    state = ((mast_hbm, mast_v, nmast_hbm), (mom1_hbm, mom1_v, nmom1_hbm), (mom2_hbm, mom2_v, nmom2_hbm))
    for i, (src, dst, _) in enumerate(state):
        pltpu.make_async_copy(src, dst, mom_sem.at[i]).start()

    barrier = pltpu.get_barrier_semaphore()

    def greet_slot(k):
        pl.semaphore_signal(barrier, inc=1, device_id=(slot_peer(k), me_h), device_id_type=MESH)

    def greet_hid(k):
        pl.semaphore_signal(barrier, inc=1, device_id=(me_s, hid_peer(k)), device_id_type=MESH)

    loop(1, slots, greet_slot)
    loop(1, hids, greet_hid)

    count = fwd_v.shape[0]
    named = jnp.broadcast_to(route_ref[...].astype(F32), (count, count))
    first = lax.broadcasted_iota(jnp.int32, (count, count), 0)
    second = lax.broadcasted_iota(jnp.int32, (count, count), 1)
    before = (named == jnp.transpose(named)) & (first < second)
    rank = jnp.sum(jnp.where(before, 1.0, 0.0), axis=0, keepdims=True)
    place = named[:1] * cap + rank
    spot = lax.broadcasted_iota(jnp.int32, (taken, count), 0).astype(F32)
    place_map = jnp.where(spot == place, 1.0, 0.0)
    back_map[...] = jnp.transpose(place_map).astype(BF16)
    fwd_load.wait()
    rows_in[...] = (
        jnp.dot(place_map.astype(BF16), fwd_v[...], preferred_element_type=F32)
        .astype(BF16)
        .reshape(slots, cap, quarter)
    )
    pl.semaphore_wait(barrier, slots + hids - 2)

    def row_copy(to):
        return remote(
            rows_in.at[to], rows_full.at[me_h, me_s], row_ss.at[to], row_rs.at[me_s], slot=to
        )

    loop(1, slots, lambda k: row_copy(slot_peer(k)).start())
    rows_full[me_h, me_s] = rows_in[me_s]

    w_load.wait()

    def first_half(c):
        for copy in xr_copies(c):
            copy.wait()
        at = pl.ds(pl.multiple_of(c * ROW_STEP, ROW_STEP), ROW_STEP)
        xc = x_v[at, :]
        rc = r_v[at, :]
        mixing_w = w_v[:2].reshape(2 * units, width)
        both = lax.dot_general(mixing_w, xc, ACROSS, preferred_element_type=F32)
        gate, up = both[:units], both[units:]
        turn = lax.dot_general(w_v[2], rc, ACROSS, preferred_element_type=F32)
        sig = jax.nn.sigmoid(gate)
        act = gate * sig
        hidden = (act * up).astype(BF16).astype(F32)
        part_v[:, at] = jnp.sum(hidden * turn, axis=0, keepdims=True)
        pre_gate[:, at] = turn * up * sig * (1.0 + gate * (1.0 - sig))
        pre_up[:, at] = turn * act
        hid_v[:, at] = hidden

    loop(0, steps, first_half)

    def part_copy(to):
        return remote(part_v, part_all.at[me_h], part_ss.at[to], part_rs.at[me_h], hid=to)

    loop(1, hids, lambda k: part_copy(hid_peer(k)).start())
    part_all[me_h] = part_v[...]

    def part_wait(k):
        frm = hid_peer(k)
        remote(part_v, part_all.at[frm], part_ss.at[frm], part_rs.at[frm], hid=frm).wait_recv()

    loop(1, hids, part_wait)
    policy = part_all[0]
    for h in range(1, hids):
        policy = policy + part_all[h]
    scores = policy - ref_ref[...]
    tot_v[...] = jnp.broadcast_to(jnp.sum(scores, axis=1, keepdims=True), tot_v.shape)

    def tot_copy(to):
        return remote(tot_v, tot_all.at[me_s], tot_ss.at[to], tot_rs.at[me_s], slot=to)

    loop(1, slots, lambda k: tot_copy(slot_peer(k)).start())
    tot_all[me_s] = tot_v[...]

    def tot_wait(k):
        frm = slot_peer(k)
        remote(tot_v, tot_all.at[frm], tot_ss.at[frm], tot_rs.at[frm], slot=frm).wait_recv()

    loop(1, slots, tot_wait)
    total = tot_all[0]
    for s in range(1, slots):
        total = total + tot_all[s]
    center = total[:, :1] * (1.0 / (slots * rows))
    slope = kto_slope(scores, label_ref[...], center)

    for s in range(slots):
        units = pl.ds(s * owned, owned)
        both = jnp.concatenate([pre_gate[units, :] * slope, pre_up[units, :] * slope], axis=0)
        d_gu[pl.ds(s * pair, pair), :] = both.astype(BF16)
    d_hid[...] = (hid_v[...] * slope).astype(BF16)

    def grad_copy(p, to):
        return remote(
            gsend.at[p, to], grecv.at[p, me_s], g_ss.at[p, to], g_rs.at[p, me_s], slot=to
        )

    def send_grads(p):
        loop(1, slots, lambda k: grad_copy(p, slot_peer(k)).start())
        grecv[p, me_s] = gsend[p, me_s]

    def mixing_grads(p):
        at = pl.ds(pl.multiple_of(p * quarter, quarter), quarter)
        found = jnp.dot(d_gu[...], x_v[:, at], preferred_element_type=F32)
        gsend[p] = found.astype(BF16).reshape(slots, pair, quarter)
        send_grads(p)

    def down_grads(p):
        low = pl.ds(pl.multiple_of((p - mixing) * quarter, quarter), quarter)
        high = pl.ds(pl.multiple_of(half + (p - mixing) * quarter, quarter), quarter)
        low_part = jnp.dot(d_hid[...], r_v[:, low], preferred_element_type=F32)
        high_part = jnp.dot(d_hid[...], r_v[:, high], preferred_element_type=F32)
        both = jnp.concatenate(
            [low_part.reshape(slots, owned, quarter), high_part.reshape(slots, owned, quarter)],
            axis=1,
        )
        gsend[p] = both.astype(BF16)
        send_grads(p)

    loop(0, mixing, mixing_grads)
    loop(mixing, pieces, down_grads)

    def row_wait(k):
        frm = slot_peer(k)
        remote(
            rows_in.at[frm], rows_full.at[me_h, frm], row_ss.at[frm], row_rs.at[frm], slot=frm
        ).wait_recv()

    loop(1, slots, row_wait)

    def gather_copy(to):
        return remote(
            rows_full.at[me_h], rows_full.at[me_h], gat_ss.at[to], gat_rs.at[me_h], hid=to
        )

    loop(1, hids, lambda k: gather_copy(hid_peer(k)).start())

    for i, (src, dst, _) in enumerate(state):
        pltpu.make_async_copy(src, dst, mom_sem.at[i]).wait()
    cur = [place_cur[s] for s in range(slots)]
    nxt = [place_next[s] for s in range(slots)]
    is_cur = [[jnp.where(cur[s] == e, 1.0, 0.0) for s in range(slots)] for e in range(experts)]
    is_nxt = [[jnp.where(nxt[t] == e, 1.0, 0.0) for t in range(slots)] for e in range(experts)]
    blocks = width // 128
    part_blocks = quarter // 128

    def weight_copy(p, to):
        return remote(
            wsend.at[p, to], wrecv.at[p, me_s], w_ss.at[p, to], w_rs.at[p, me_s], slot=to
        )

    def adam(p, spots):
        def grad_wait(k):
            frm = slot_peer(k)
            remote(
                gsend.at[p, frm], grecv.at[p, frm], g_ss.at[p, frm], g_rs.at[p, frm], slot=frm
            ).wait_recv()

        loop(1, slots, grad_wait)

        def lane_block(j):
            lanes = pl.ds(pl.multiple_of(j * 128, 128), 128)
            came = [grecv[p, s, :, lanes].astype(F32) for s in range(slots)]
            fresh = []
            for e in range(experts):
                summed = came[0] * is_cur[e][0]
                for s in range(1, slots):
                    summed = summed + came[s] * is_cur[e][s]
                sides = []
                for side, (kind, block) in enumerate(spots(j)):
                    row = e * 3 + kind
                    at = pl.ds(block, owned, stride=blocks)
                    new_m, new_1, new_2 = adamw_update(
                        mast_v[row, at, :],
                        mom1_v[row, at, :],
                        mom2_v[row, at, :],
                        summed[side * owned : (side + 1) * owned],
                    )
                    mast_v[row, at, :] = new_m
                    mom1_v[row, at, :] = new_1
                    mom2_v[row, at, :] = new_2
                    sides.append(new_m)
                fresh.append(jnp.concatenate(sides, axis=0))
            for t in range(slots):
                chosen = fresh[0] * is_nxt[0][t]
                for e in range(1, experts):
                    chosen = chosen + fresh[e] * is_nxt[e][t]
                wsend[p, t, :, lanes] = chosen.astype(BF16)

        loop(0, part_blocks, lane_block)
        loop(1, slots, lambda k: weight_copy(p, slot_peer(k)).start())
        wrecv[p, me_s] = wsend[p, me_s]

    def mixing_adam(p):
        adam(p, lambda j: [(side, p * part_blocks + j) for side in range(2)])

    def down_adam(p):
        start = (p - mixing) * part_blocks
        adam(p, lambda j: [(2, side * (blocks // 2) + start + j) for side in range(2)])

    loop(0, mixing, mixing_adam)
    loop(mixing, pieces, down_adam)
    for i, (_, dst, new) in enumerate(state):
        pltpu.make_async_copy(dst, new, store_sem.at[i]).start()

    def gather_wait(k):
        frm = hid_peer(k)
        remote(
            rows_full.at[frm], rows_full.at[frm], gat_ss.at[frm], gat_rs.at[frm], hid=frm
        ).wait_recv()

    loop(1, hids, gather_wait)

    def weight_wait(p):
        def one(k):
            frm = slot_peer(k)
            remote(
                wsend.at[p, frm], wrecv.at[p, frm], w_ss.at[p, frm], w_rs.at[p, frm], slot=frm
            ).wait_recv()

        loop(1, slots, one)

    mixed = None
    for h in range(hids):
        weight_wait(h)
        term = lax.dot_general(
            wrecv[h].reshape(slots * pair, quarter),
            rows_full[h].reshape(taken, quarter),
            ACROSS,
            preferred_element_type=F32,
        )
        mixed = term if mixed is None else mixed + term
    mixed = mixed.reshape(slots, pair, taken)
    gate = mixed[:, :owned]
    hidden = gate * jax.nn.sigmoid(gate) * mixed[:, owned:]
    blank = jnp.zeros_like(hidden)
    low_hid = jnp.concatenate([hidden, blank], axis=1).reshape(slots * pair, taken)
    high_hid = jnp.concatenate([blank, hidden], axis=1).reshape(slots * pair, taken)
    side_hid[0] = jnp.transpose(low_hid).astype(BF16)
    side_hid[1] = jnp.transpose(high_hid).astype(BF16)

    pos = lax.rem(me_h, 2)
    grp = me_h // 2
    mate = grp * 2 + 1 - pos
    far = (1 - grp) * 2 + pos

    def lev1_copy(g, turn):
        return remote(out_part.at[2 * g + turn], lev1.at[g], l1_ss.at[g], l1_rs.at[g], hid=mate)

    def lev2_copy(s):
        return remote(lev2_send.at[s], lev2.at[s], l2_ss.at[s], l2_rs.at[s], hid=far)

    def ret_copy(to):
        return remote(
            ret_send.at[to], ret_recv.at[me_s], ret_ss.at[to], ret_rs.at[me_s], slot=to
        )

    def to_far(k):
        s = slot_peer(k)
        both = out_part[far, s].astype(F32) + lev1[1 - grp, s].astype(F32)
        lev2_send[s] = both.astype(BF16)
        lev2_copy(s).start()

    def last_sum(s):
        lev2_copy(s).wait_recv()
        own = out_part[me_h, s].astype(F32) + lev1[grp, s].astype(F32)
        return (own + lev2[s].astype(F32)).astype(BF16)

    def give_back(k):
        s = slot_peer(k)
        ret_send[s] = last_sum(s)
        ret_copy(s).start()

    for turn in range(2):
        weight_wait(mixing + turn)
        for i in range(2):
            g = 1 - grp if i == 0 else grp
            got = jnp.dot(
                side_hid[g],
                wrecv[mixing + turn].reshape(slots * pair, quarter),
                preferred_element_type=F32,
            )
            out_part[2 * g + turn] = got.astype(BF16).reshape(slots, cap, quarter)

            @pl.when(pos != turn)
            def _(g=g, turn=turn):
                lev1_copy(g, turn).start()

        @pl.when(pos == turn)
        def _(turn=turn):
            lev1_copy(1 - grp, turn).wait_recv()
            loop(1, slots + 1, to_far)
            lev1_copy(grp, turn).wait_recv()
            loop(1, slots, give_back)
            ret_recv[me_s] = last_sum(me_s)

    def ret_wait(k):
        frm = slot_peer(k)
        remote(
            ret_send.at[frm], ret_recv.at[frm], ret_ss.at[frm], ret_rs.at[frm], slot=frm
        ).wait_recv()

    loop(1, slots, ret_wait)
    fwd_v[...] = jnp.dot(
        back_map[...], ret_recv[...].reshape(taken, quarter), preferred_element_type=F32
    ).astype(BF16)
    out_store = pltpu.make_async_copy(fwd_v, out_hbm, load_sem.at[1])
    out_store.start()

    def slot_sends(k):
        to = slot_peer(k)
        row_copy(to).wait_send()
        tot_copy(to).wait_send()
        for p in range(pieces):
            grad_copy(p, to).wait_send()
            weight_copy(p, to).wait_send()
        ret_copy(to).wait_send()

    def hid_sends(k):
        to = hid_peer(k)
        part_copy(to).wait_send()
        gather_copy(to).wait_send()

    loop(1, slots, slot_sends)
    loop(1, hids, hid_sends)
    loop(0, slots, lambda s: lev2_copy(s).wait_send())
    for g in range(2):
        lev1_copy(g, 1 - pos).wait_send()
    out_store.wait()
    for i, (_, dst, new) in enumerate(state):
        pltpu.make_async_copy(dst, new, store_sem.at[i]).wait()


def results_kernel(rows_in, mast_in, mom1_in, mom2_in, rows_out, mast_out, mom1_out, mom2_out, sem):
    parts = sem.shape[1]
    size = mast_in.shape[0] // parts
    moves = [pltpu.make_async_copy(rows_in, rows_out, sem.at[3, 0])]
    for c in range(parts):
        at = pl.ds(c * size, size)
        for i, (src, dst) in enumerate(
            ((mast_in, mast_out), (mom1_in, mom1_out), (mom2_in, mom2_out))
        ):
            moves.append(pltpu.make_async_copy(src.at[at], dst.at[at], sem.at[i, c]))
    for move in moves:
        move.start()
    for move in moves:
        move.wait()


def fused_shards(
    master,
    first_moment,
    second_moment,
    slot_weights,
    back_rows,
    readout,
    ref_logratio,
    labels,
    place_cur,
    place_next,
    fwd_rows,
    routes,
):
    slots = lax.axis_size("slot")
    hids = lax.axis_size("hid")
    experts = master.shape[0]
    _, kinds, units, width = slot_weights.shape
    owned = units // slots
    rows = back_rows.shape[1]
    half = width // 2
    quarter = fwd_rows.shape[1]
    cap = 2 * fwd_rows.shape[0] // slots
    taken = slots * cap
    lines = (experts * kinds, owned * width // 128, 128)
    vmem = pl.BlockSpec(memory_space=pltpu.VMEM)
    smem = pl.BlockSpec(memory_space=pltpu.SMEM)
    anywhere = pl.BlockSpec(memory_space=pl.ANY)
    pieces = (width // quarter + half // quarter, slots, 2 * owned, quarter)
    dma = pltpu.SemaphoreType.DMA
    scratch = [
        pltpu.VMEM(fwd_rows.shape, BF16),
        pltpu.VMEM((slots, cap, quarter), BF16),
        pltpu.VMEM((fwd_rows.shape[0], taken), BF16),
        pltpu.VMEM((kinds, units, width), BF16),
        pltpu.VMEM((rows, width), BF16),
        pltpu.VMEM((rows, width), BF16),
        pltpu.VMEM(lines, F32),
        pltpu.VMEM(lines, F32),
        pltpu.VMEM(lines, F32),
        pltpu.VMEM((units, rows), F32),
        pltpu.VMEM((units, rows), F32),
        pltpu.VMEM((units, rows), F32),
        pltpu.VMEM((2 * units, rows), BF16),
        pltpu.VMEM((units, rows), BF16),
        pltpu.VMEM(pieces, BF16),
        pltpu.VMEM(pieces, BF16),
        pltpu.VMEM(pieces, BF16),
        pltpu.VMEM(pieces, BF16),
        pltpu.VMEM((hids, slots, cap, quarter), BF16),
        pltpu.VMEM((1, rows), F32),
        pltpu.VMEM((hids, 1, rows), F32),
        pltpu.VMEM((1, 128), F32),
        pltpu.VMEM((slots, 1, 128), F32),
        pltpu.VMEM((2, taken, 2 * units), BF16),
        pltpu.VMEM((hids, slots, cap, quarter), BF16),
        pltpu.VMEM((2, slots, cap, quarter), BF16),
        pltpu.VMEM((slots, cap, quarter), BF16),
        pltpu.VMEM((slots, cap, quarter), BF16),
        pltpu.VMEM((slots, cap, quarter), BF16),
        pltpu.VMEM((slots, cap, quarter), BF16),
        dma((2,)),
        dma((2, rows // ROW_STEP)),
        dma((3,)),
        dma((3,)),
        dma((slots,)),
        dma((slots,)),
        dma((hids,)),
        dma((hids,)),
        dma((hids,)),
        dma((hids,)),
        dma((slots,)),
        dma((slots,)),
        dma(pieces[:2]),
        dma(pieces[:2]),
        dma(pieces[:2]),
        dma(pieces[:2]),
        dma((2,)),
        dma((2,)),
        dma((slots,)),
        dma((slots,)),
        dma((slots,)),
        dma((slots,)),
    ]
    state_shape = jax.ShapeDtypeStruct(lines, F32)
    out_rows, new_master, new_first, new_second = pl.pallas_call(
        functools.partial(kto_kernel, slots, hids, owned, experts),
        out_shape=(
            jax.ShapeDtypeStruct(fwd_rows.shape, BF16),
            state_shape,
            state_shape,
            state_shape,
        ),
        in_specs=[smem, smem, vmem, vmem, vmem] + [anywhere] * 7,
        out_specs=(anywhere,) * 4,
        scratch_shapes=scratch,
        compiler_params=pltpu.CompilerParams(
            collective_id=0, has_side_effects=True, vmem_limit_bytes=VMEM_BYTES
        ),
        cost_estimate=pl.CostEstimate(
            flops=2 * (6 * rows + 3 * taken) * units * width,
            bytes_accessed=24 * master.size + 4 * rows * width,
            transcendentals=2 * rows * units,
        ),
    )(
        place_cur,
        place_next,
        routes.reshape(1, fwd_rows.shape[0]),
        labels,
        ref_logratio,
        fwd_rows,
        slot_weights[0],
        back_rows[0],
        readout[0],
        master.reshape(lines),
        first_moment.reshape(lines),
        second_moment.reshape(lines),
    )
    out_rows, new_master, new_first, new_second = pl.pallas_call(
        results_kernel,
        out_shape=(
            jax.ShapeDtypeStruct(fwd_rows.shape, BF16),
            state_shape,
            state_shape,
            state_shape,
        ),
        in_specs=[anywhere] * 4,
        out_specs=(anywhere,) * 4,
        scratch_shapes=[dma((4, experts))],
        compiler_params=pltpu.CompilerParams(vmem_limit_bytes=8 * 1024 * 1024),
        cost_estimate=pl.CostEstimate(
            flops=0, bytes_accessed=24 * master.size, transcendentals=0
        ),
    )(out_rows, new_master, new_first, new_second)
    shape = master.shape
    return (out_rows, new_master.reshape(shape), new_first.reshape(shape), new_second.reshape(shape))


VMEM_BYTES = 46 * 1024 * 1024


def step(*arrays):
    slots = lax.axis_size("slot")
    weights, fwd_rows = arrays[3], arrays[10]
    owned = weights.shape[2] // slots
    cap = 2 * fwd_rows.shape[0] // slots
    fits = owned % 8 == 0 and cap % 16 == 0 and lax.axis_size("hid") == 4
    fits = fits and weights.shape[3] == 4 * fwd_rows.shape[1] and weights.shape[3] % 1024 == 0
    fits = fits and arrays[4].shape[1] % ROW_STEP == 0
    return (fused_shards if fits else shards)(*arrays)


def solution(mesh):
    return jax.shard_map(
        step,
        mesh=mesh,
        in_specs=(
            P(None, None, "hid", "slot"),
            P(None, None, "hid", "slot"),
            P(None, None, "hid", "slot"),
            P("slot", None, "hid", None),
            P("slot", None, None),
            P("slot", None, None),
            P("slot", None),
            P("slot", None),
            P(),
            P(),
            P("slot", "hid"),
            P("slot", None),
        ),
        out_specs=(
            P("slot", "hid"),
            P(None, None, "hid", "slot"),
            P(None, None, "hid", "slot"),
            P(None, None, "hid", "slot"),
        ),
        check_vma=False,
    )
```

```python
import functools

import jax
import jax.numpy as jnp
from jax import lax
from jax.experimental import pallas as pl
from jax.experimental.pallas import tpu as pltpu
from jax.sharding import PartitionSpec as P

beta_kto = 1.0
desired_weight = 1.0
undesired_weight = 1.33
learn_rate = 0.004
decay_first = 0.9
decay_second = 0.999
correct_first = 0.9999734386011124
correct_second = 0.09520785288629043
adam_eps = 1e-08
weight_decay = 0.1


def expert_pass(inputs, weights):
    across = (((1,), (1,)), ((), ()))
    gate_vals = lax.dot_general(inputs, weights[0], across, preferred_element_type=jnp.float32)
    up_vals = lax.dot_general(inputs, weights[1], across, preferred_element_type=jnp.float32)
    hidden = (gate_vals * jax.nn.sigmoid(gate_vals) * up_vals).astype(jnp.bfloat16)
    produced = jnp.dot(hidden, weights[2], preferred_element_type=jnp.float32)
    return (gate_vals, up_vals, hidden, produced)


def kto_slope(scores, labels, center):
    sigma_v = jax.nn.sigmoid(beta_kto * (scores - center))
    signed = jnp.where(labels == 1, -desired_weight, undesired_weight)
    return beta_kto * sigma_v * (1.0 - sigma_v) * signed


def expert_backward(inputs, direction, weights, slope, gate_vals, up_vals, hidden):
    d_expert = (slope[:, None] * direction.astype(jnp.float32)).astype(jnp.bfloat16)
    d_hidden = lax.dot_general(
        d_expert, weights[2], (((1,), (1,)), ((), ())), preferred_element_type=jnp.float32
    )
    sigma_g = jax.nn.sigmoid(gate_vals)
    d_gate = (d_hidden * up_vals * sigma_g * (1.0 + gate_vals * (1.0 - sigma_g))).astype(
        jnp.bfloat16
    )
    d_up = (d_hidden * gate_vals * sigma_g).astype(jnp.bfloat16)
    contract = (((0,), (0,)), ((), ()))
    grad_gate = lax.dot_general(d_gate, inputs, contract, preferred_element_type=jnp.float32)
    grad_up = lax.dot_general(d_up, inputs, contract, preferred_element_type=jnp.float32)
    grad_down = lax.dot_general(hidden, d_expert, contract, preferred_element_type=jnp.float32)
    return jnp.stack([grad_gate, grad_up, grad_down])


def adamw_update(master, first_moment, second_moment, summed):
    new_first = decay_first * first_moment + (1.0 - decay_first) * summed
    new_second = decay_second * second_moment + (1.0 - decay_second) * summed * summed
    update = new_first / correct_first / (jnp.sqrt(new_second / correct_second) + adam_eps)
    new_master = master - learn_rate * (update + weight_decay * master)
    return (new_master, new_first, new_second)


def shards(
    master,
    first_moment,
    second_moment,
    slot_weights,
    back_rows,
    readout,
    ref_logratio,
    labels,
    place_cur,
    place_next,
    fwd_rows,
    routes,
):
    slot_count = lax.axis_size("slot")
    experts_here = master.shape[0]
    weights = slot_weights[0]
    width = weights.shape[2]
    owned_units = master.shape[3] // width
    inputs = back_rows[0]
    direction = readout[0]
    gate_vals, up_vals, hidden, partial_value = expert_pass(inputs, weights)
    row_part = jnp.sum(partial_value * direction.astype(jnp.float32), axis=1)
    policy = lax.psum(row_part, "hid")
    scores = policy - ref_logratio[0]
    row_total = slot_count * inputs.shape[0]
    center = lax.psum(jnp.sum(scores), "slot") / row_total
    slope = kto_slope(scores, labels[0], center)
    grads = expert_backward(inputs, direction, weights, slope, gate_vals, up_vals, hidden)
    arrived = lax.all_to_all(
        grads[None].astype(jnp.bfloat16), "slot", split_axis=2, concat_axis=0, tiled=True
    ).astype(jnp.float32)
    arrived = arrived.reshape(slot_count, 3, 1, owned_units * width)
    owner_map = (place_cur[None, :] == jnp.arange(experts_here, dtype=jnp.int32)[:, None]).astype(
        jnp.float32
    )
    summed = jnp.einsum("es,sabc->eabc", owner_map, arrived, precision=lax.Precision.HIGHEST)
    new_master, new_first, new_second = adamw_update(master, first_moment, second_moment, summed)
    refreshed = new_master.astype(jnp.bfloat16)
    pick_map = (place_next[:, None] == jnp.arange(experts_here, dtype=jnp.int32)[None, :]).astype(
        jnp.bfloat16
    )
    picked = jnp.einsum(
        "se,eabc->sabc", pick_map, refreshed, preferred_element_type=jnp.float32
    ).astype(jnp.bfloat16)
    picked = picked.reshape(slot_count, 3, owned_units, width)
    resident = lax.all_to_all(picked, "slot", split_axis=0, concat_axis=2, tiled=True)[0]
    capacity = 2 * fwd_rows.shape[0] // slot_count
    quarter = fwd_rows.shape[1]
    target = routes[:, 0]
    target_map = (target[:, None] == jnp.arange(slot_count, dtype=jnp.int32)[None, :]).astype(
        jnp.int32
    )
    earlier = jnp.cumsum(target_map, axis=0) - target_map
    position = jnp.sum(earlier * target_map, axis=1)
    slot_place = target * capacity + position
    place_map = (
        slot_place[None, :] == jnp.arange(slot_count * capacity, dtype=jnp.int32)[:, None]
    ).astype(jnp.bfloat16)
    buffer_rows = jnp.dot(place_map, fwd_rows, preferred_element_type=jnp.float32).astype(
        jnp.bfloat16
    )
    buffer_rows = buffer_rows.reshape(slot_count, capacity, quarter)
    arrived_rows = lax.all_to_all(
        buffer_rows, "slot", split_axis=0, concat_axis=0, tiled=True
    ).reshape(slot_count * capacity, quarter)
    across = (((1,), (1,)), ((), ()))
    piece_rows = lax.all_gather(arrived_rows, "hid", axis=1, tiled=True)
    gate_cols = resident[0]
    up_cols = resident[1]
    fwd_gate = lax.dot_general(piece_rows, gate_cols, across, preferred_element_type=jnp.float32)
    fwd_up = lax.dot_general(piece_rows, up_cols, across, preferred_element_type=jnp.float32)
    fwd_hidden = (fwd_gate * jax.nn.sigmoid(fwd_gate) * fwd_up).astype(jnp.bfloat16)
    fwd_partial = jnp.dot(fwd_hidden, resident[2], preferred_element_type=jnp.float32)
    totals = lax.psum(fwd_partial, "hid")
    shares = lax.dynamic_slice_in_dim(totals, lax.axis_index("hid") * quarter, quarter, 1)
    outgoing = shares.astype(jnp.bfloat16).reshape(slot_count, capacity, quarter)
    returned = lax.all_to_all(outgoing, "slot", split_axis=0, concat_axis=0, tiled=True).reshape(
        slot_count * capacity, quarter
    )
    out_rows = lax.dot_general(
        place_map, returned, (((0,), (0,)), ((), ())), preferred_element_type=jnp.float32
    ).astype(jnp.bfloat16)
    return (out_rows, new_master, new_first, new_second)


ACROSS = (((1,), (1,)), ((), ()))
F32 = jnp.float32
BF16 = jnp.bfloat16
MESH = pl.DeviceIdType.MESH
ROW_STEP = 256


def kto_kernel(
    slots,
    hids,
    owned,
    experts,
    place_cur_hbm,
    place_next_hbm,
    route_hbm,
    label_hbm,
    ref_hbm,
    fwd_hbm,
    w_hbm,
    x_hbm,
    r_hbm,
    mast_hbm,
    mom1_hbm,
    mom2_hbm,
    out_hbm,
    nmast_hbm,
    nmom1_hbm,
    nmom2_hbm,
    place_cur,
    place_next,
    route_ref,
    label_ref,
    ref_ref,
    fwd_v,
    rows_in,
    back_map,
    w_v,
    x_v,
    r_v,
    mast_v,
    mom1_v,
    mom2_v,
    pre_gate,
    pre_up,
    hid_v,
    d_gu,
    d_hid,
    gsend,
    grecv,
    wsend,
    wrecv,
    rows_full,
    part_v,
    part_all,
    tot_v,
    tot_all,
    side_hid,
    out_part,
    lev1,
    lev2_send,
    lev2,
    ret_send,
    ret_recv,
    load_sem,
    small_sem,
    xr_sem,
    mom_sem,
    store_sem,
    row_ss,
    row_rs,
    gat_ss,
    gat_rs,
    part_ss,
    part_rs,
    tot_ss,
    tot_rs,
    g_ss,
    g_rs,
    w_ss,
    w_rs,
    l1_ss,
    l1_rs,
    l2_ss,
    l2_rs,
    ret_ss,
    ret_rs,
):
    me_s = lax.axis_index("slot")
    me_h = lax.axis_index("hid")
    units, width = w_v.shape[1:]
    half = width // 2
    quarter = rows_in.shape[2]
    cap = rows_in.shape[1]
    taken = slots * cap
    pair = 2 * owned
    rows = x_v.shape[0]
    mixing = width // quarter
    pieces = mixing + half // quarter
    steps = rows // ROW_STEP

    def flipped(bits):
        found, unit = 0, 1
        while unit < slots:
            bit = lax.rem(me_s // unit, 2)
            found = found + unit * (1 - bit if bits // unit % 2 else bit)
            unit *= 2
        return found

    across_middle = list(range(slots // 2, slots))
    near = list(range(1, slots // 2))
    turns = across_middle[:1]
    for i, bits in enumerate(near):
        turns += [bits, across_middle[i + 1]]
    partners = [flipped(bits) for bits in turns] + [me_s]

    def slot_peer(k):
        return partners[k - 1]

    def hid_peer(k):
        return lax.rem(me_h + k, hids)

    def remote(src, dst, ssem, rsem, slot=None, hid=None):
        return pltpu.make_async_remote_copy(
            src_ref=src,
            dst_ref=dst,
            send_sem=ssem,
            recv_sem=rsem,
            device_id=(me_s if slot is None else slot, me_h if hid is None else hid),
            device_id_type=MESH,
        )

    def loop(low, high, body):
        def step(i, carry):
            body(i)
            return carry

        lax.fori_loop(low, high, step, 0)

    def each(low, high, body):
        for k in range(low, high):
            body(k)

    fwd_load = pltpu.make_async_copy(fwd_hbm, fwd_v, load_sem.at[1])
    fwd_load.start()
    small = [
        pltpu.make_async_copy(src, dst, small_sem.at[i])
        for i, (src, dst) in enumerate(
            (
                (route_hbm, route_ref),
                (label_hbm, label_ref),
                (ref_hbm, ref_ref),
                (place_cur_hbm, place_cur),
                (place_next_hbm, place_next),
            )
        )
    ]
    for copy in small:
        copy.start()
    w_load = pltpu.make_async_copy(w_hbm, w_v, load_sem.at[0])
    w_load.start()

    def xr_copies(c):
        at = pl.ds(pl.multiple_of(c * ROW_STEP, ROW_STEP), ROW_STEP)
        return (
            pltpu.make_async_copy(x_hbm.at[at], x_v.at[at], xr_sem.at[0, c]),
            pltpu.make_async_copy(r_hbm.at[at], r_v.at[at], xr_sem.at[1, c]),
        )

    def start_xr(c):
        for copy in xr_copies(c):
            copy.start()

    loop(0, steps, start_xr)
    state = ((mast_hbm, mast_v, nmast_hbm), (mom1_hbm, mom1_v, nmom1_hbm), (mom2_hbm, mom2_v, nmom2_hbm))
    for i, (src, dst, _) in enumerate(state):
        pltpu.make_async_copy(src, dst, mom_sem.at[i]).start()

    barrier = pltpu.get_barrier_semaphore()

    def greet_slot(k):
        pl.semaphore_signal(barrier, inc=1, device_id=(slot_peer(k), me_h), device_id_type=MESH)

    def greet_hid(k):
        pl.semaphore_signal(barrier, inc=1, device_id=(me_s, hid_peer(k)), device_id_type=MESH)

    each(1, slots, greet_slot)
    loop(1, hids, greet_hid)

    for copy in small:
        copy.wait()
    count = fwd_v.shape[0]
    named = jnp.broadcast_to(route_ref[...].astype(F32), (count, count))
    first = lax.broadcasted_iota(jnp.int32, (count, count), 0)
    second = lax.broadcasted_iota(jnp.int32, (count, count), 1)
    before = (named == jnp.transpose(named)) & (first < second)
    rank = jnp.sum(jnp.where(before, 1.0, 0.0), axis=0, keepdims=True)
    place = named[:1] * cap + rank
    spot = lax.broadcasted_iota(jnp.int32, (taken, count), 0).astype(F32)
    place_map = jnp.where(spot == place, 1.0, 0.0)
    back_map[...] = jnp.transpose(place_map).astype(BF16)
    fwd_load.wait()
    rows_in[...] = (
        jnp.dot(place_map.astype(BF16), fwd_v[...], preferred_element_type=F32)
        .astype(BF16)
        .reshape(slots, cap, quarter)
    )
    pl.semaphore_wait(barrier, slots + hids - 2)

    def row_copy(to):
        return remote(
            rows_in.at[to], rows_full.at[me_h, me_s], row_ss.at[to], row_rs.at[me_s], slot=to
        )

    each(1, slots, lambda k: row_copy(slot_peer(k)).start())
    rows_full[me_h, me_s] = rows_in[me_s]

    w_load.wait()

    def first_half(c):
        for copy in xr_copies(c):
            copy.wait()
        at = pl.ds(pl.multiple_of(c * ROW_STEP, ROW_STEP), ROW_STEP)
        xc = x_v[at, :]
        rc = r_v[at, :]
        mixing_w = w_v[:2].reshape(2 * units, width)
        both = lax.dot_general(mixing_w, xc, ACROSS, preferred_element_type=F32)
        gate, up = both[:units], both[units:]
        turn = lax.dot_general(w_v[2], rc, ACROSS, preferred_element_type=F32)
        sig = jax.nn.sigmoid(gate)
        act = gate * sig
        hidden = (act * up).astype(BF16).astype(F32)
        part_v[:, at] = jnp.sum(hidden * turn, axis=0, keepdims=True)
        pre_gate[:, at] = turn * up * sig * (1.0 + gate * (1.0 - sig))
        pre_up[:, at] = turn * act
        hid_v[:, at] = hidden

    loop(0, steps, first_half)

    def part_copy(to):
        return remote(part_v, part_all.at[me_h], part_ss.at[to], part_rs.at[me_h], hid=to)

    loop(1, hids, lambda k: part_copy(hid_peer(k)).start())
    part_all[me_h] = part_v[...]

    def part_wait(k):
        frm = hid_peer(k)
        remote(part_v, part_all.at[frm], part_ss.at[frm], part_rs.at[frm], hid=frm).wait_recv()

    loop(1, hids, part_wait)
    policy = part_all[0]
    for h in range(1, hids):
        policy = policy + part_all[h]
    scores = policy - ref_ref[...]
    tot_v[...] = jnp.broadcast_to(jnp.sum(scores, axis=1, keepdims=True), tot_v.shape)

    def tot_copy(to):
        return remote(tot_v, tot_all.at[me_s], tot_ss.at[to], tot_rs.at[me_s], slot=to)

    each(1, slots, lambda k: tot_copy(slot_peer(k)).start())
    tot_all[me_s] = tot_v[...]

    def tot_wait(k):
        frm = slot_peer(k)
        remote(tot_v, tot_all.at[frm], tot_ss.at[frm], tot_rs.at[frm], slot=frm).wait_recv()

    each(1, slots, tot_wait)
    total = tot_all[0]
    for s in range(1, slots):
        total = total + tot_all[s]
    center = total[:, :1] * (1.0 / (slots * rows))
    slope = kto_slope(scores, label_ref[...], center)

    for s in range(slots):
        units = pl.ds(s * owned, owned)
        both = jnp.concatenate([pre_gate[units, :] * slope, pre_up[units, :] * slope], axis=0)
        d_gu[pl.ds(s * pair, pair), :] = both.astype(BF16)
    d_hid[...] = (hid_v[...] * slope).astype(BF16)

    def grad_copy(p, to):
        return remote(
            gsend.at[p, to], grecv.at[p, me_s], g_ss.at[p, to], g_rs.at[p, me_s], slot=to
        )

    def send_grads(p):
        each(1, slots, lambda k: grad_copy(p, slot_peer(k)).start())
        grecv[p, me_s] = gsend[p, me_s]

    def mixing_grads(p):
        at = pl.ds(pl.multiple_of(p * quarter, quarter), quarter)
        found = jnp.dot(d_gu[...], x_v[:, at], preferred_element_type=F32)
        gsend[p] = found.astype(BF16).reshape(slots, pair, quarter)
        send_grads(p)

    def down_grads(p):
        low = pl.ds(pl.multiple_of((p - mixing) * quarter, quarter), quarter)
        high = pl.ds(pl.multiple_of(half + (p - mixing) * quarter, quarter), quarter)
        low_part = jnp.dot(d_hid[...], r_v[:, low], preferred_element_type=F32)
        high_part = jnp.dot(d_hid[...], r_v[:, high], preferred_element_type=F32)
        both = jnp.concatenate(
            [low_part.reshape(slots, owned, quarter), high_part.reshape(slots, owned, quarter)],
            axis=1,
        )
        gsend[p] = both.astype(BF16)
        send_grads(p)

    loop(0, mixing, mixing_grads)
    loop(mixing, pieces, down_grads)

    def row_wait(k):
        frm = slot_peer(k)
        remote(
            rows_in.at[frm], rows_full.at[me_h, frm], row_ss.at[frm], row_rs.at[frm], slot=frm
        ).wait_recv()

    each(1, slots, row_wait)

    def gather_copy(to):
        return remote(
            rows_full.at[me_h], rows_full.at[me_h], gat_ss.at[to], gat_rs.at[me_h], hid=to
        )

    loop(1, hids, lambda k: gather_copy(hid_peer(k)).start())

    for i, (src, dst, _) in enumerate(state):
        pltpu.make_async_copy(src, dst, mom_sem.at[i]).wait()
    cur = [place_cur[s] for s in range(slots)]
    nxt = [place_next[s] for s in range(slots)]
    is_cur = [[jnp.where(cur[s] == e, 1.0, 0.0) for s in range(slots)] for e in range(experts)]
    is_nxt = [[jnp.where(nxt[t] == e, 1.0, 0.0) for t in range(slots)] for e in range(experts)]
    blocks = width // 128
    part_blocks = quarter // 128

    def weight_copy(p, to):
        return remote(
            wsend.at[p, to], wrecv.at[p, me_s], w_ss.at[p, to], w_rs.at[p, me_s], slot=to
        )

    def adam(p, spots):
        def grad_wait(k):
            frm = slot_peer(k)
            remote(
                gsend.at[p, frm], grecv.at[p, frm], g_ss.at[p, frm], g_rs.at[p, frm], slot=frm
            ).wait_recv()

        each(1, slots, grad_wait)

        def lane_block(j):
            lanes = pl.ds(pl.multiple_of(j * 128, 128), 128)
            came = [grecv[p, s, :, lanes].astype(F32) for s in range(slots)]
            fresh = []
            for e in range(experts):
                summed = came[0] * is_cur[e][0]
                for s in range(1, slots):
                    summed = summed + came[s] * is_cur[e][s]
                sides = []
                for side, (kind, block) in enumerate(spots(j)):
                    row = e * 3 + kind
                    at = pl.ds(block, owned, stride=blocks)
                    new_m, new_1, new_2 = adamw_update(
                        mast_v[row, at, :],
                        mom1_v[row, at, :],
                        mom2_v[row, at, :],
                        summed[side * owned : (side + 1) * owned],
                    )
                    mast_v[row, at, :] = new_m
                    mom1_v[row, at, :] = new_1
                    mom2_v[row, at, :] = new_2
                    sides.append(new_m)
                fresh.append(jnp.concatenate(sides, axis=0))
            for t in range(slots):
                chosen = fresh[0] * is_nxt[0][t]
                for e in range(1, experts):
                    chosen = chosen + fresh[e] * is_nxt[e][t]
                wsend[p, t, :, lanes] = chosen.astype(BF16)

        loop(0, part_blocks, lane_block)
        each(1, slots, lambda k: weight_copy(p, slot_peer(k)).start())
        wrecv[p, me_s] = wsend[p, me_s]

    def mixing_adam(p):
        adam(p, lambda j: [(side, p * part_blocks + j) for side in range(2)])

    def down_adam(p):
        start = (p - mixing) * part_blocks
        adam(p, lambda j: [(2, side * (blocks // 2) + start + j) for side in range(2)])

    loop(0, mixing, mixing_adam)
    loop(mixing, pieces, down_adam)
    for i, (_, dst, new) in enumerate(state):
        pltpu.make_async_copy(dst, new, store_sem.at[i]).start()

    def gather_wait(k):
        frm = hid_peer(k)
        remote(
            rows_full.at[frm], rows_full.at[frm], gat_ss.at[frm], gat_rs.at[frm], hid=frm
        ).wait_recv()

    loop(1, hids, gather_wait)

    def weight_wait(p):
        def one(k):
            frm = slot_peer(k)
            remote(
                wsend.at[p, frm], wrecv.at[p, frm], w_ss.at[p, frm], w_rs.at[p, frm], slot=frm
            ).wait_recv()

        each(1, slots, one)

    mixed = None
    for h in range(hids):
        weight_wait(h)
        term = lax.dot_general(
            wrecv[h].reshape(slots * pair, quarter),
            rows_full[h].reshape(taken, quarter),
            ACROSS,
            preferred_element_type=F32,
        )
        mixed = term if mixed is None else mixed + term
    mixed = mixed.reshape(slots, pair, taken)
    gate = mixed[:, :owned]
    hidden = gate * jax.nn.sigmoid(gate) * mixed[:, owned:]
    blank = jnp.zeros_like(hidden)
    low_hid = jnp.concatenate([hidden, blank], axis=1).reshape(slots * pair, taken)
    high_hid = jnp.concatenate([blank, hidden], axis=1).reshape(slots * pair, taken)
    side_hid[0] = jnp.transpose(low_hid).astype(BF16)
    side_hid[1] = jnp.transpose(high_hid).astype(BF16)

    pos = lax.rem(me_h, 2)
    grp = me_h // 2
    mate = grp * 2 + 1 - pos
    far = (1 - grp) * 2 + pos

    def lev1_copy(g, turn):
        return remote(out_part.at[2 * g + turn], lev1.at[g], l1_ss.at[g], l1_rs.at[g], hid=mate)

    def lev2_copy(s):
        return remote(lev2_send.at[s], lev2.at[s], l2_ss.at[s], l2_rs.at[s], hid=far)

    def ret_copy(to):
        return remote(
            ret_send.at[to], ret_recv.at[me_s], ret_ss.at[to], ret_rs.at[me_s], slot=to
        )

    def to_far(k):
        s = slot_peer(k)
        both = out_part[far, s].astype(F32) + lev1[1 - grp, s].astype(F32)
        lev2_send[s] = both.astype(BF16)
        lev2_copy(s).start()

    def last_sum(s):
        lev2_copy(s).wait_recv()
        own = out_part[me_h, s].astype(F32) + lev1[grp, s].astype(F32)
        return (own + lev2[s].astype(F32)).astype(BF16)

    def give_back(k):
        s = slot_peer(k)
        ret_send[s] = last_sum(s)
        ret_copy(s).start()

    for turn in range(2):
        weight_wait(mixing + turn)
        for i in range(2):
            g = 1 - grp if i == 0 else grp
            got = jnp.dot(
                side_hid[g],
                wrecv[mixing + turn].reshape(slots * pair, quarter),
                preferred_element_type=F32,
            )
            out_part[2 * g + turn] = got.astype(BF16).reshape(slots, cap, quarter)

            @pl.when(pos != turn)
            def _(g=g, turn=turn):
                lev1_copy(g, turn).start()

        @pl.when(pos == turn)
        def _(turn=turn):
            lev1_copy(1 - grp, turn).wait_recv()
            each(1, slots + 1, to_far)
            lev1_copy(grp, turn).wait_recv()
            each(1, slots, give_back)
            ret_recv[me_s] = last_sum(me_s)

    def ret_wait(k):
        frm = slot_peer(k)
        remote(
            ret_send.at[frm], ret_recv.at[frm], ret_ss.at[frm], ret_rs.at[frm], slot=frm
        ).wait_recv()

    each(1, slots, ret_wait)
    fwd_v[...] = jnp.dot(
        back_map[...], ret_recv[...].reshape(taken, quarter), preferred_element_type=F32
    ).astype(BF16)
    out_store = pltpu.make_async_copy(fwd_v, out_hbm, load_sem.at[1])
    out_store.start()

    def slot_sends(k):
        to = slot_peer(k)
        row_copy(to).wait_send()
        tot_copy(to).wait_send()
        for p in range(pieces):
            grad_copy(p, to).wait_send()
            weight_copy(p, to).wait_send()
        ret_copy(to).wait_send()

    def hid_sends(k):
        to = hid_peer(k)
        part_copy(to).wait_send()
        gather_copy(to).wait_send()

    each(1, slots, slot_sends)
    loop(1, hids, hid_sends)
    loop(0, slots, lambda s: lev2_copy(s).wait_send())
    for g in range(2):
        lev1_copy(g, 1 - pos).wait_send()
    out_store.wait()
    for i, (_, dst, new) in enumerate(state):
        pltpu.make_async_copy(dst, new, store_sem.at[i]).wait()


def results_kernel(rows_in, mast_in, mom1_in, mom2_in, rows_out, mast_out, mom1_out, mom2_out, sem):
    parts = sem.shape[1]
    size = mast_in.shape[0] // parts
    moves = [pltpu.make_async_copy(rows_in, rows_out, sem.at[3, 0])]
    for c in range(parts):
        at = pl.ds(c * size, size)
        for i, (src, dst) in enumerate(
            ((mast_in, mast_out), (mom1_in, mom1_out), (mom2_in, mom2_out))
        ):
            moves.append(pltpu.make_async_copy(src.at[at], dst.at[at], sem.at[i, c]))
    for move in moves:
        move.start()
    for move in moves:
        move.wait()


def fused_shards(
    master,
    first_moment,
    second_moment,
    slot_weights,
    back_rows,
    readout,
    ref_logratio,
    labels,
    place_cur,
    place_next,
    fwd_rows,
    routes,
):
    slots = lax.axis_size("slot")
    hids = lax.axis_size("hid")
    experts = master.shape[0]
    _, kinds, units, width = slot_weights.shape
    owned = units // slots
    rows = back_rows.shape[1]
    half = width // 2
    quarter = fwd_rows.shape[1]
    cap = 2 * fwd_rows.shape[0] // slots
    taken = slots * cap
    lines = (experts * kinds, owned * width // 128, 128)
    pinned = pl.BlockSpec(memory_space=pltpu.HBM)
    anywhere = pl.BlockSpec(memory_space=pl.ANY)
    pieces = (width // quarter + half // quarter, slots, 2 * owned, quarter)
    dma = pltpu.SemaphoreType.DMA
    scratch = [
        pltpu.SMEM(place_cur.shape, jnp.int32),
        pltpu.SMEM(place_next.shape, jnp.int32),
        pltpu.VMEM((1, fwd_rows.shape[0]), jnp.int32),
        pltpu.VMEM(labels.shape, jnp.int32),
        pltpu.VMEM(ref_logratio.shape, F32),
        pltpu.VMEM(fwd_rows.shape, BF16),
        pltpu.VMEM((slots, cap, quarter), BF16),
        pltpu.VMEM((fwd_rows.shape[0], taken), BF16),
        pltpu.VMEM((kinds, units, width), BF16),
        pltpu.VMEM((rows, width), BF16),
        pltpu.VMEM((rows, width), BF16),
        pltpu.VMEM(lines, F32),
        pltpu.VMEM(lines, F32),
        pltpu.VMEM(lines, F32),
        pltpu.VMEM((units, rows), F32),
        pltpu.VMEM((units, rows), F32),
        pltpu.VMEM((units, rows), F32),
        pltpu.VMEM((2 * units, rows), BF16),
        pltpu.VMEM((units, rows), BF16),
        pltpu.VMEM(pieces, BF16),
        pltpu.VMEM(pieces, BF16),
        pltpu.VMEM(pieces, BF16),
        pltpu.VMEM(pieces, BF16),
        pltpu.VMEM((hids, slots, cap, quarter), BF16),
        pltpu.VMEM((1, rows), F32),
        pltpu.VMEM((hids, 1, rows), F32),
        pltpu.VMEM((1, 128), F32),
        pltpu.VMEM((slots, 1, 128), F32),
        pltpu.VMEM((2, taken, 2 * units), BF16),
        pltpu.VMEM((hids, slots, cap, quarter), BF16),
        pltpu.VMEM((2, slots, cap, quarter), BF16),
        pltpu.VMEM((slots, cap, quarter), BF16),
        pltpu.VMEM((slots, cap, quarter), BF16),
        pltpu.VMEM((slots, cap, quarter), BF16),
        pltpu.VMEM((slots, cap, quarter), BF16),
        dma((2,)),
        dma((5,)),
        dma((2, rows // ROW_STEP)),
        dma((3,)),
        dma((3,)),
        dma((slots,)),
        dma((slots,)),
        dma((hids,)),
        dma((hids,)),
        dma((hids,)),
        dma((hids,)),
        dma((slots,)),
        dma((slots,)),
        dma(pieces[:2]),
        dma(pieces[:2]),
        dma(pieces[:2]),
        dma(pieces[:2]),
        dma((2,)),
        dma((2,)),
        dma((slots,)),
        dma((slots,)),
        dma((slots,)),
        dma((slots,)),
    ]
    state_shape = jax.ShapeDtypeStruct(lines, F32)
    out_rows, new_master, new_first, new_second = pl.pallas_call(
        functools.partial(kto_kernel, slots, hids, owned, experts),
        out_shape=(
            jax.ShapeDtypeStruct(fwd_rows.shape, BF16),
            state_shape,
            state_shape,
            state_shape,
        ),
        in_specs=[pinned] * 12,
        out_specs=(anywhere,) * 4,
        scratch_shapes=scratch,
        compiler_params=pltpu.CompilerParams(
            collective_id=0, has_side_effects=True, vmem_limit_bytes=VMEM_BYTES
        ),
        cost_estimate=pl.CostEstimate(
            flops=2 * (6 * rows + 3 * taken) * units * width,
            bytes_accessed=24 * master.size + 4 * rows * width,
            transcendentals=2 * rows * units,
        ),
    )(
        place_cur,
        place_next,
        routes.reshape(1, fwd_rows.shape[0]),
        labels,
        ref_logratio,
        fwd_rows,
        slot_weights[0],
        back_rows[0],
        readout[0],
        master.reshape(lines),
        first_moment.reshape(lines),
        second_moment.reshape(lines),
    )
    out_rows, new_master, new_first, new_second = pl.pallas_call(
        results_kernel,
        out_shape=(
            jax.ShapeDtypeStruct(fwd_rows.shape, BF16),
            state_shape,
            state_shape,
            state_shape,
        ),
        in_specs=[anywhere] * 4,
        out_specs=(anywhere,) * 4,
        scratch_shapes=[dma((4, experts))],
        compiler_params=pltpu.CompilerParams(vmem_limit_bytes=VMEM_BYTES),
        cost_estimate=pl.CostEstimate(
            flops=0, bytes_accessed=24 * master.size, transcendentals=0
        ),
    )(out_rows, new_master, new_first, new_second)
    shape = master.shape
    return (out_rows, new_master.reshape(shape), new_first.reshape(shape), new_second.reshape(shape))


VMEM_BYTES = 60 * 1024 * 1024


def step(*arrays):
    slots = lax.axis_size("slot")
    weights, fwd_rows = arrays[3], arrays[10]
    owned = weights.shape[2] // slots
    cap = 2 * fwd_rows.shape[0] // slots
    fits = owned % 8 == 0 and cap % 16 == 0 and lax.axis_size("hid") == 4
    fits = fits and slots & (slots - 1) == 0
    fits = fits and weights.shape[3] == 4 * fwd_rows.shape[1] and weights.shape[3] % 1024 == 0
    fits = fits and arrays[4].shape[1] % ROW_STEP == 0
    return (fused_shards if fits else shards)(*arrays)


def solution(mesh):
    return jax.shard_map(
        step,
        mesh=mesh,
        in_specs=(
            P(None, None, "hid", "slot"),
            P(None, None, "hid", "slot"),
            P(None, None, "hid", "slot"),
            P("slot", None, "hid", None),
            P("slot", None, None),
            P("slot", None, None),
            P("slot", None),
            P("slot", None),
            P(),
            P(),
            P("slot", "hid"),
            P("slot", None),
        ),
        out_specs=(
            P("slot", "hid"),
            P(None, None, "hid", "slot"),
            P(None, None, "hid", "slot"),
            P(None, None, "hid", "slot"),
        ),
        check_vma=False,
    )
```

```python
import functools

import jax
import jax.numpy as jnp
from jax import lax
from jax.experimental import pallas as pl
from jax.experimental.pallas import tpu as pltpu
from jax.sharding import PartitionSpec as P

beta_kto = 1.0
desired_weight = 1.0
undesired_weight = 1.33
learn_rate = 0.004
decay_first = 0.9
decay_second = 0.999
correct_first = 0.9999734386011124
correct_second = 0.09520785288629043
adam_eps = 1e-08
weight_decay = 0.1


def expert_pass(inputs, weights):
    across = (((1,), (1,)), ((), ()))
    gate_vals = lax.dot_general(inputs, weights[0], across, preferred_element_type=jnp.float32)
    up_vals = lax.dot_general(inputs, weights[1], across, preferred_element_type=jnp.float32)
    hidden = (gate_vals * jax.nn.sigmoid(gate_vals) * up_vals).astype(jnp.bfloat16)
    produced = jnp.dot(hidden, weights[2], preferred_element_type=jnp.float32)
    return (gate_vals, up_vals, hidden, produced)


def kto_slope(scores, labels, center):
    sigma_v = jax.nn.sigmoid(beta_kto * (scores - center))
    signed = jnp.where(labels == 1, -desired_weight, undesired_weight)
    return beta_kto * sigma_v * (1.0 - sigma_v) * signed


def expert_backward(inputs, direction, weights, slope, gate_vals, up_vals, hidden):
    d_expert = (slope[:, None] * direction.astype(jnp.float32)).astype(jnp.bfloat16)
    d_hidden = lax.dot_general(
        d_expert, weights[2], (((1,), (1,)), ((), ())), preferred_element_type=jnp.float32
    )
    sigma_g = jax.nn.sigmoid(gate_vals)
    d_gate = (d_hidden * up_vals * sigma_g * (1.0 + gate_vals * (1.0 - sigma_g))).astype(
        jnp.bfloat16
    )
    d_up = (d_hidden * gate_vals * sigma_g).astype(jnp.bfloat16)
    contract = (((0,), (0,)), ((), ()))
    grad_gate = lax.dot_general(d_gate, inputs, contract, preferred_element_type=jnp.float32)
    grad_up = lax.dot_general(d_up, inputs, contract, preferred_element_type=jnp.float32)
    grad_down = lax.dot_general(hidden, d_expert, contract, preferred_element_type=jnp.float32)
    return jnp.stack([grad_gate, grad_up, grad_down])


def adamw_update(master, first_moment, second_moment, summed):
    new_first = decay_first * first_moment + (1.0 - decay_first) * summed
    new_second = decay_second * second_moment + (1.0 - decay_second) * summed * summed
    update = new_first / correct_first / (jnp.sqrt(new_second / correct_second) + adam_eps)
    new_master = master - learn_rate * (update + weight_decay * master)
    return (new_master, new_first, new_second)


def shards(
    master,
    first_moment,
    second_moment,
    slot_weights,
    back_rows,
    readout,
    ref_logratio,
    labels,
    place_cur,
    place_next,
    fwd_rows,
    routes,
):
    slot_count = lax.axis_size("slot")
    experts_here = master.shape[0]
    weights = slot_weights[0]
    width = weights.shape[2]
    owned_units = master.shape[3] // width
    inputs = back_rows[0]
    direction = readout[0]
    gate_vals, up_vals, hidden, partial_value = expert_pass(inputs, weights)
    row_part = jnp.sum(partial_value * direction.astype(jnp.float32), axis=1)
    policy = lax.psum(row_part, "hid")
    scores = policy - ref_logratio[0]
    row_total = slot_count * inputs.shape[0]
    center = lax.psum(jnp.sum(scores), "slot") / row_total
    slope = kto_slope(scores, labels[0], center)
    grads = expert_backward(inputs, direction, weights, slope, gate_vals, up_vals, hidden)
    arrived = lax.all_to_all(
        grads[None].astype(jnp.bfloat16), "slot", split_axis=2, concat_axis=0, tiled=True
    ).astype(jnp.float32)
    arrived = arrived.reshape(slot_count, 3, 1, owned_units * width)
    owner_map = (place_cur[None, :] == jnp.arange(experts_here, dtype=jnp.int32)[:, None]).astype(
        jnp.float32
    )
    summed = jnp.einsum("es,sabc->eabc", owner_map, arrived, precision=lax.Precision.HIGHEST)
    new_master, new_first, new_second = adamw_update(master, first_moment, second_moment, summed)
    refreshed = new_master.astype(jnp.bfloat16)
    pick_map = (place_next[:, None] == jnp.arange(experts_here, dtype=jnp.int32)[None, :]).astype(
        jnp.bfloat16
    )
    picked = jnp.einsum(
        "se,eabc->sabc", pick_map, refreshed, preferred_element_type=jnp.float32
    ).astype(jnp.bfloat16)
    picked = picked.reshape(slot_count, 3, owned_units, width)
    resident = lax.all_to_all(picked, "slot", split_axis=0, concat_axis=2, tiled=True)[0]
    capacity = 2 * fwd_rows.shape[0] // slot_count
    quarter = fwd_rows.shape[1]
    target = routes[:, 0]
    target_map = (target[:, None] == jnp.arange(slot_count, dtype=jnp.int32)[None, :]).astype(
        jnp.int32
    )
    earlier = jnp.cumsum(target_map, axis=0) - target_map
    position = jnp.sum(earlier * target_map, axis=1)
    slot_place = target * capacity + position
    place_map = (
        slot_place[None, :] == jnp.arange(slot_count * capacity, dtype=jnp.int32)[:, None]
    ).astype(jnp.bfloat16)
    buffer_rows = jnp.dot(place_map, fwd_rows, preferred_element_type=jnp.float32).astype(
        jnp.bfloat16
    )
    buffer_rows = buffer_rows.reshape(slot_count, capacity, quarter)
    arrived_rows = lax.all_to_all(
        buffer_rows, "slot", split_axis=0, concat_axis=0, tiled=True
    ).reshape(slot_count * capacity, quarter)
    across = (((1,), (1,)), ((), ()))
    piece_rows = lax.all_gather(arrived_rows, "hid", axis=1, tiled=True)
    gate_cols = resident[0]
    up_cols = resident[1]
    fwd_gate = lax.dot_general(piece_rows, gate_cols, across, preferred_element_type=jnp.float32)
    fwd_up = lax.dot_general(piece_rows, up_cols, across, preferred_element_type=jnp.float32)
    fwd_hidden = (fwd_gate * jax.nn.sigmoid(fwd_gate) * fwd_up).astype(jnp.bfloat16)
    fwd_partial = jnp.dot(fwd_hidden, resident[2], preferred_element_type=jnp.float32)
    totals = lax.psum(fwd_partial, "hid")
    shares = lax.dynamic_slice_in_dim(totals, lax.axis_index("hid") * quarter, quarter, 1)
    outgoing = shares.astype(jnp.bfloat16).reshape(slot_count, capacity, quarter)
    returned = lax.all_to_all(outgoing, "slot", split_axis=0, concat_axis=0, tiled=True).reshape(
        slot_count * capacity, quarter
    )
    out_rows = lax.dot_general(
        place_map, returned, (((0,), (0,)), ((), ())), preferred_element_type=jnp.float32
    ).astype(jnp.bfloat16)
    return (out_rows, new_master, new_first, new_second)


ACROSS = (((1,), (1,)), ((), ()))
F32 = jnp.float32
BF16 = jnp.bfloat16
MESH = pl.DeviceIdType.MESH
ROW_STEP = 256


def kto_kernel(
    slots,
    hids,
    owned,
    experts,
    ints_ref,
    ref_ref,
    fwd_hbm,
    w_hbm,
    x_hbm,
    r_hbm,
    mast_hbm,
    mom1_hbm,
    mom2_hbm,
    out_hbm,
    nmast_hbm,
    nmom1_hbm,
    nmom2_hbm,
    ints,
    fwd_v,
    rows_in,
    back_map,
    w_v,
    x_v,
    r_v,
    mast_v,
    mom1_v,
    mom2_v,
    pre_gate,
    pre_up,
    hid_v,
    d_gu,
    d_hid,
    gsend,
    grecv,
    wsend,
    wrecv,
    rows_full,
    part_v,
    part_all,
    tot_v,
    tot_all,
    side_hid,
    out_part,
    lev1,
    lev2_send,
    lev2,
    ret_send,
    ret_recv,
    load_sem,
    ints_sem,
    xr_sem,
    mom_sem,
    store_sem,
    row_ss,
    row_rs,
    gat_ss,
    gat_rs,
    part_ss,
    part_rs,
    tot_ss,
    tot_rs,
    g_ss,
    g_rs,
    w_ss,
    w_rs,
    l1_ss,
    l1_rs,
    l2_ss,
    l2_rs,
    ret_ss,
    ret_rs,
):
    me_s = lax.axis_index("slot")
    me_h = lax.axis_index("hid")
    units, width = w_v.shape[1:]
    half = width // 2
    quarter = rows_in.shape[2]
    cap = rows_in.shape[1]
    taken = slots * cap
    pair = 2 * owned
    rows = x_v.shape[0]
    mixing = width // quarter
    pieces = mixing + half // quarter
    steps = rows // ROW_STEP

    def slot_peer(k):
        return lax.rem(me_s + k, slots)

    def hid_peer(k):
        return lax.rem(me_h + k, hids)

    def remote(src, dst, ssem, rsem, slot=None, hid=None):
        return pltpu.make_async_remote_copy(
            src_ref=src,
            dst_ref=dst,
            send_sem=ssem,
            recv_sem=rsem,
            device_id=(me_s if slot is None else slot, me_h if hid is None else hid),
            device_id_type=MESH,
        )

    def loop(low, high, body):
        def step(i, carry):
            body(i)
            return carry

        lax.fori_loop(low, high, step, 0)

    fwd_load = pltpu.make_async_copy(fwd_hbm, fwd_v, load_sem.at[1])
    fwd_load.start()
    ints_load = pltpu.make_async_copy(ints_ref, ints, ints_sem.at[0])
    ints_load.start()
    w_load = pltpu.make_async_copy(w_hbm, w_v, load_sem.at[0])
    w_load.start()

    def xr_copies(c):
        at = pl.ds(pl.multiple_of(c * ROW_STEP, ROW_STEP), ROW_STEP)
        return (
            pltpu.make_async_copy(x_hbm.at[at], x_v.at[at], xr_sem.at[0, c]),
            pltpu.make_async_copy(r_hbm.at[at], r_v.at[at], xr_sem.at[1, c]),
        )

    def start_xr(c):
        for copy in xr_copies(c):
            copy.start()

    loop(0, steps, start_xr)
    state = ((mast_hbm, mast_v, nmast_hbm), (mom1_hbm, mom1_v, nmom1_hbm), (mom2_hbm, mom2_v, nmom2_hbm))
    for i, (src, dst, _) in enumerate(state):
        pltpu.make_async_copy(src, dst, mom_sem.at[i]).start()

    barrier = pltpu.get_barrier_semaphore()

    def greet_slot(k):
        pl.semaphore_signal(barrier, inc=1, device_id=(slot_peer(k), me_h), device_id_type=MESH)

    def greet_hid(k):
        pl.semaphore_signal(barrier, inc=1, device_id=(me_s, hid_peer(k)), device_id_type=MESH)

    loop(1, slots, greet_slot)
    loop(1, hids, greet_hid)

    count = fwd_v.shape[0]
    targets = ints_ref[:, rows : rows + count].astype(F32)
    named = jnp.broadcast_to(targets, (count, count))
    first = lax.broadcasted_iota(jnp.int32, (count, count), 0)
    second = lax.broadcasted_iota(jnp.int32, (count, count), 1)
    before = (named == jnp.transpose(named)) & (first < second)
    rank = jnp.sum(jnp.where(before, 1.0, 0.0), axis=0, keepdims=True)
    place = named[:1] * cap + rank
    spot = lax.broadcasted_iota(jnp.int32, (taken, count), 0).astype(F32)
    place_map = jnp.where(spot == place, 1.0, 0.0)
    back_map[...] = jnp.transpose(place_map).astype(BF16)
    fwd_load.wait()
    rows_in[...] = (
        jnp.dot(place_map.astype(BF16), fwd_v[...], preferred_element_type=F32)
        .astype(BF16)
        .reshape(slots, cap, quarter)
    )
    pl.semaphore_wait(barrier, slots + hids - 2)

    def row_copy(to):
        return remote(
            rows_in.at[to], rows_full.at[me_h, me_s], row_ss.at[to], row_rs.at[me_s], slot=to
        )

    loop(1, slots, lambda k: row_copy(slot_peer(k)).start())
    rows_full[me_h, me_s] = rows_in[me_s]

    w_load.wait()

    def first_half(c):
        for copy in xr_copies(c):
            copy.wait()
        at = pl.ds(pl.multiple_of(c * ROW_STEP, ROW_STEP), ROW_STEP)
        xc = x_v[at, :]
        rc = r_v[at, :]
        mixing_w = w_v[:2].reshape(2 * units, width)
        both = lax.dot_general(mixing_w, xc, ACROSS, preferred_element_type=F32)
        gate, up = both[:units], both[units:]
        turn = lax.dot_general(w_v[2], rc, ACROSS, preferred_element_type=F32)
        sig = jax.nn.sigmoid(gate)
        act = gate * sig
        hidden = (act * up).astype(BF16).astype(F32)
        part_v[:, at] = jnp.sum(hidden * turn, axis=0, keepdims=True)
        pre_gate[:, at] = turn * up * sig * (1.0 + gate * (1.0 - sig))
        pre_up[:, at] = turn * act
        hid_v[:, at] = hidden

    loop(0, steps, first_half)

    def part_copy(to):
        return remote(part_v, part_all.at[me_h], part_ss.at[to], part_rs.at[me_h], hid=to)

    loop(1, hids, lambda k: part_copy(hid_peer(k)).start())
    part_all[me_h] = part_v[...]

    def part_wait(k):
        frm = hid_peer(k)
        remote(part_v, part_all.at[frm], part_ss.at[frm], part_rs.at[frm], hid=frm).wait_recv()

    loop(1, hids, part_wait)
    policy = part_all[0]
    for h in range(1, hids):
        policy = policy + part_all[h]
    scores = policy - ref_ref[...]
    tot_v[...] = jnp.broadcast_to(jnp.sum(scores, axis=1, keepdims=True), tot_v.shape)

    def tot_copy(to):
        return remote(tot_v, tot_all.at[me_s], tot_ss.at[to], tot_rs.at[me_s], slot=to)

    loop(1, slots, lambda k: tot_copy(slot_peer(k)).start())
    tot_all[me_s] = tot_v[...]

    def tot_wait(k):
        frm = slot_peer(k)
        remote(tot_v, tot_all.at[frm], tot_ss.at[frm], tot_rs.at[frm], slot=frm).wait_recv()

    loop(1, slots, tot_wait)
    total = tot_all[0]
    for s in range(1, slots):
        total = total + tot_all[s]
    center = total[:, :1] * (1.0 / (slots * rows))
    slope = kto_slope(scores, ints_ref[:, :rows], center)

    for s in range(slots):
        units = pl.ds(s * owned, owned)
        both = jnp.concatenate([pre_gate[units, :] * slope, pre_up[units, :] * slope], axis=0)
        d_gu[pl.ds(s * pair, pair), :] = both.astype(BF16)
    d_hid[...] = (hid_v[...] * slope).astype(BF16)

    def grad_copy(p, to):
        return remote(
            gsend.at[p, to], grecv.at[p, me_s], g_ss.at[p, to], g_rs.at[p, me_s], slot=to
        )

    def send_grads(p):
        loop(1, slots, lambda k: grad_copy(p, slot_peer(k)).start())
        grecv[p, me_s] = gsend[p, me_s]

    def mixing_grads(p):
        at = pl.ds(pl.multiple_of(p * quarter, quarter), quarter)
        found = jnp.dot(d_gu[...], x_v[:, at], preferred_element_type=F32)
        gsend[p] = found.astype(BF16).reshape(slots, pair, quarter)
        send_grads(p)

    def down_grads(p):
        low = pl.ds(pl.multiple_of((p - mixing) * quarter, quarter), quarter)
        high = pl.ds(pl.multiple_of(half + (p - mixing) * quarter, quarter), quarter)
        low_part = jnp.dot(d_hid[...], r_v[:, low], preferred_element_type=F32)
        high_part = jnp.dot(d_hid[...], r_v[:, high], preferred_element_type=F32)
        both = jnp.concatenate(
            [low_part.reshape(slots, owned, quarter), high_part.reshape(slots, owned, quarter)],
            axis=1,
        )
        gsend[p] = both.astype(BF16)
        send_grads(p)

    loop(0, mixing, mixing_grads)
    loop(mixing, pieces, down_grads)

    def row_wait(k):
        frm = slot_peer(k)
        remote(
            rows_in.at[frm], rows_full.at[me_h, frm], row_ss.at[frm], row_rs.at[frm], slot=frm
        ).wait_recv()

    loop(1, slots, row_wait)

    def gather_copy(to):
        return remote(
            rows_full.at[me_h], rows_full.at[me_h], gat_ss.at[to], gat_rs.at[me_h], hid=to
        )

    loop(1, hids, lambda k: gather_copy(hid_peer(k)).start())

    for i, (src, dst, _) in enumerate(state):
        pltpu.make_async_copy(src, dst, mom_sem.at[i]).wait()
    ints_load.wait()
    places = rows + count
    cur = [ints[0, places + s] for s in range(slots)]
    nxt = [ints[0, places + slots + s] for s in range(slots)]
    is_cur = [[jnp.where(cur[s] == e, 1.0, 0.0) for s in range(slots)] for e in range(experts)]
    is_nxt = [[jnp.where(nxt[t] == e, 1.0, 0.0) for t in range(slots)] for e in range(experts)]
    blocks = width // 128
    part_blocks = quarter // 128

    def weight_copy(p, to):
        return remote(
            wsend.at[p, to], wrecv.at[p, me_s], w_ss.at[p, to], w_rs.at[p, me_s], slot=to
        )

    def adam(p, spots):
        def grad_wait(k):
            frm = slot_peer(k)
            remote(
                gsend.at[p, frm], grecv.at[p, frm], g_ss.at[p, frm], g_rs.at[p, frm], slot=frm
            ).wait_recv()

        loop(1, slots, grad_wait)

        def lane_block(j):
            lanes = pl.ds(pl.multiple_of(j * 128, 128), 128)
            came = [grecv[p, s, :, lanes].astype(F32) for s in range(slots)]
            fresh = []
            for e in range(experts):
                summed = came[0] * is_cur[e][0]
                for s in range(1, slots):
                    summed = summed + came[s] * is_cur[e][s]
                sides = []
                for side, (kind, block) in enumerate(spots(j)):
                    row = e * 3 + kind
                    at = pl.ds(block, owned, stride=blocks)
                    new_m, new_1, new_2 = adamw_update(
                        mast_v[row, at, :],
                        mom1_v[row, at, :],
                        mom2_v[row, at, :],
                        summed[side * owned : (side + 1) * owned],
                    )
                    mast_v[row, at, :] = new_m
                    mom1_v[row, at, :] = new_1
                    mom2_v[row, at, :] = new_2
                    sides.append(new_m)
                fresh.append(jnp.concatenate(sides, axis=0))
            for t in range(slots):
                chosen = fresh[0] * is_nxt[0][t]
                for e in range(1, experts):
                    chosen = chosen + fresh[e] * is_nxt[e][t]
                wsend[p, t, :, lanes] = chosen.astype(BF16)

        loop(0, part_blocks, lane_block)
        loop(1, slots, lambda k: weight_copy(p, slot_peer(k)).start())
        wrecv[p, me_s] = wsend[p, me_s]

    def mixing_adam(p):
        adam(p, lambda j: [(side, p * part_blocks + j) for side in range(2)])

    def down_adam(p):
        start = (p - mixing) * part_blocks
        adam(p, lambda j: [(2, side * (blocks // 2) + start + j) for side in range(2)])

    loop(0, mixing, mixing_adam)
    loop(mixing, pieces, down_adam)
    for i, (_, dst, new) in enumerate(state):
        pltpu.make_async_copy(dst, new, store_sem.at[i]).start()

    def gather_wait(k):
        frm = hid_peer(k)
        remote(
            rows_full.at[frm], rows_full.at[frm], gat_ss.at[frm], gat_rs.at[frm], hid=frm
        ).wait_recv()

    loop(1, hids, gather_wait)

    def weight_wait(p):
        def one(k):
            frm = slot_peer(k)
            remote(
                wsend.at[p, frm], wrecv.at[p, frm], w_ss.at[p, frm], w_rs.at[p, frm], slot=frm
            ).wait_recv()

        loop(1, slots, one)

    mixed = None
    for h in range(hids):
        weight_wait(h)
        term = lax.dot_general(
            wrecv[h].reshape(slots * pair, quarter),
            rows_full[h].reshape(taken, quarter),
            ACROSS,
            preferred_element_type=F32,
        )
        mixed = term if mixed is None else mixed + term
    mixed = mixed.reshape(slots, pair, taken)
    gate = mixed[:, :owned]
    hidden = gate * jax.nn.sigmoid(gate) * mixed[:, owned:]
    blank = jnp.zeros_like(hidden)
    low_hid = jnp.concatenate([hidden, blank], axis=1).reshape(slots * pair, taken)
    high_hid = jnp.concatenate([blank, hidden], axis=1).reshape(slots * pair, taken)
    side_hid[0] = jnp.transpose(low_hid).astype(BF16)
    side_hid[1] = jnp.transpose(high_hid).astype(BF16)

    pos = lax.rem(me_h, 2)
    grp = me_h // 2
    mate = grp * 2 + 1 - pos
    far = (1 - grp) * 2 + pos

    def lev1_copy(g, turn):
        return remote(out_part.at[2 * g + turn], lev1.at[g], l1_ss.at[g], l1_rs.at[g], hid=mate)

    def lev2_copy(s):
        return remote(lev2_send.at[s], lev2.at[s], l2_ss.at[s], l2_rs.at[s], hid=far)

    def ret_copy(to):
        return remote(
            ret_send.at[to], ret_recv.at[me_s], ret_ss.at[to], ret_rs.at[me_s], slot=to
        )

    def to_far(k):
        s = slot_peer(k)
        both = out_part[far, s].astype(F32) + lev1[1 - grp, s].astype(F32)
        lev2_send[s] = both.astype(BF16)
        lev2_copy(s).start()

    def last_sum(s):
        lev2_copy(s).wait_recv()
        own = out_part[me_h, s].astype(F32) + lev1[grp, s].astype(F32)
        return (own + lev2[s].astype(F32)).astype(BF16)

    def give_back(k):
        s = slot_peer(k)
        ret_send[s] = last_sum(s)
        ret_copy(s).start()

    for turn in range(2):
        weight_wait(mixing + turn)
        for i in range(2):
            g = 1 - grp if i == 0 else grp
            got = jnp.dot(
                side_hid[g],
                wrecv[mixing + turn].reshape(slots * pair, quarter),
                preferred_element_type=F32,
            )
            out_part[2 * g + turn] = got.astype(BF16).reshape(slots, cap, quarter)

            @pl.when(pos != turn)
            def _(g=g, turn=turn):
                lev1_copy(g, turn).start()

        @pl.when(pos == turn)
        def _(turn=turn):
            lev1_copy(1 - grp, turn).wait_recv()
            loop(1, slots + 1, to_far)
            lev1_copy(grp, turn).wait_recv()
            loop(1, slots, give_back)
            ret_recv[me_s] = last_sum(me_s)

    def ret_wait(k):
        frm = slot_peer(k)
        remote(
            ret_send.at[frm], ret_recv.at[frm], ret_ss.at[frm], ret_rs.at[frm], slot=frm
        ).wait_recv()

    loop(1, slots, ret_wait)
    fwd_v[...] = jnp.dot(
        back_map[...], ret_recv[...].reshape(taken, quarter), preferred_element_type=F32
    ).astype(BF16)
    out_store = pltpu.make_async_copy(fwd_v, out_hbm, load_sem.at[1])
    out_store.start()

    def slot_sends(k):
        to = slot_peer(k)
        row_copy(to).wait_send()
        tot_copy(to).wait_send()
        for p in range(pieces):
            grad_copy(p, to).wait_send()
            weight_copy(p, to).wait_send()
        ret_copy(to).wait_send()

    def hid_sends(k):
        to = hid_peer(k)
        part_copy(to).wait_send()
        gather_copy(to).wait_send()

    loop(1, slots, slot_sends)
    loop(1, hids, hid_sends)
    loop(0, slots, lambda s: lev2_copy(s).wait_send())
    for g in range(2):
        lev1_copy(g, 1 - pos).wait_send()
    out_store.wait()
    for i, (_, dst, new) in enumerate(state):
        pltpu.make_async_copy(dst, new, store_sem.at[i]).wait()


def results_kernel(rows_in, mast_in, mom1_in, mom2_in, rows_out, mast_out, mom1_out, mom2_out, sem):
    parts = sem.shape[1]
    size = mast_in.shape[0] // parts
    moves = [pltpu.make_async_copy(rows_in, rows_out, sem.at[3, 0])]
    for c in range(parts):
        at = pl.ds(c * size, size)
        for i, (src, dst) in enumerate(
            ((mast_in, mast_out), (mom1_in, mom1_out), (mom2_in, mom2_out))
        ):
            moves.append(pltpu.make_async_copy(src.at[at], dst.at[at], sem.at[i, c]))
    for move in moves:
        move.start()
    for move in moves:
        move.wait()


def fused_shards(
    master,
    first_moment,
    second_moment,
    slot_weights,
    back_rows,
    readout,
    ref_logratio,
    labels,
    place_cur,
    place_next,
    fwd_rows,
    routes,
):
    slots = lax.axis_size("slot")
    hids = lax.axis_size("hid")
    experts = master.shape[0]
    _, kinds, units, width = slot_weights.shape
    owned = units // slots
    rows = back_rows.shape[1]
    half = width // 2
    quarter = fwd_rows.shape[1]
    cap = 2 * fwd_rows.shape[0] // slots
    taken = slots * cap
    ints = jnp.concatenate(
        [labels, routes.reshape(1, -1), place_cur[None], place_next[None]], axis=1
    )
    lines = (experts * kinds, owned * width // 128, 128)
    vmem = pl.BlockSpec(memory_space=pltpu.VMEM)
    anywhere = pl.BlockSpec(memory_space=pl.ANY)
    pieces = (width // quarter + half // quarter, slots, 2 * owned, quarter)
    dma = pltpu.SemaphoreType.DMA
    scratch = [
        pltpu.SMEM(ints.shape, jnp.int32),
        pltpu.VMEM(fwd_rows.shape, BF16),
        pltpu.VMEM((slots, cap, quarter), BF16),
        pltpu.VMEM((fwd_rows.shape[0], taken), BF16),
        pltpu.VMEM((kinds, units, width), BF16),
        pltpu.VMEM((rows, width), BF16),
        pltpu.VMEM((rows, width), BF16),
        pltpu.VMEM(lines, F32),
        pltpu.VMEM(lines, F32),
        pltpu.VMEM(lines, F32),
        pltpu.VMEM((units, rows), F32),
        pltpu.VMEM((units, rows), F32),
        pltpu.VMEM((units, rows), F32),
        pltpu.VMEM((2 * units, rows), BF16),
        pltpu.VMEM((units, rows), BF16),
        pltpu.VMEM(pieces, BF16),
        pltpu.VMEM(pieces, BF16),
        pltpu.VMEM(pieces, BF16),
        pltpu.VMEM(pieces, BF16),
        pltpu.VMEM((hids, slots, cap, quarter), BF16),
        pltpu.VMEM((1, rows), F32),
        pltpu.VMEM((hids, 1, rows), F32),
        pltpu.VMEM((1, 128), F32),
        pltpu.VMEM((slots, 1, 128), F32),
        pltpu.VMEM((2, taken, 2 * units), BF16),
        pltpu.VMEM((hids, slots, cap, quarter), BF16),
        pltpu.VMEM((2, slots, cap, quarter), BF16),
        pltpu.VMEM((slots, cap, quarter), BF16),
        pltpu.VMEM((slots, cap, quarter), BF16),
        pltpu.VMEM((slots, cap, quarter), BF16),
        pltpu.VMEM((slots, cap, quarter), BF16),
        dma((2,)),
        dma((1,)),
        dma((2, rows // ROW_STEP)),
        dma((3,)),
        dma((3,)),
        dma((slots,)),
        dma((slots,)),
        dma((hids,)),
        dma((hids,)),
        dma((hids,)),
        dma((hids,)),
        dma((slots,)),
        dma((slots,)),
        dma(pieces[:2]),
        dma(pieces[:2]),
        dma(pieces[:2]),
        dma(pieces[:2]),
        dma((2,)),
        dma((2,)),
        dma((slots,)),
        dma((slots,)),
        dma((slots,)),
        dma((slots,)),
    ]
    state_shape = jax.ShapeDtypeStruct(lines, F32)
    out_rows, new_master, new_first, new_second = pl.pallas_call(
        functools.partial(kto_kernel, slots, hids, owned, experts),
        out_shape=(
            jax.ShapeDtypeStruct(fwd_rows.shape, BF16),
            state_shape,
            state_shape,
            state_shape,
        ),
        in_specs=[vmem, vmem] + [anywhere] * 7,
        out_specs=(anywhere,) * 4,
        scratch_shapes=scratch,
        compiler_params=pltpu.CompilerParams(
            collective_id=0, has_side_effects=True, vmem_limit_bytes=VMEM_BYTES
        ),
        cost_estimate=pl.CostEstimate(
            flops=2 * (6 * rows + 3 * taken) * units * width,
            bytes_accessed=24 * master.size + 4 * rows * width,
            transcendentals=2 * rows * units,
        ),
    )(
        ints,
        ref_logratio,
        fwd_rows,
        slot_weights[0],
        back_rows[0],
        readout[0],
        master.reshape(lines),
        first_moment.reshape(lines),
        second_moment.reshape(lines),
    )
    out_rows, new_master, new_first, new_second = pl.pallas_call(
        results_kernel,
        out_shape=(
            jax.ShapeDtypeStruct(fwd_rows.shape, BF16),
            state_shape,
            state_shape,
            state_shape,
        ),
        in_specs=[anywhere] * 4,
        out_specs=(anywhere,) * 4,
        scratch_shapes=[dma((4, experts))],
        compiler_params=pltpu.CompilerParams(vmem_limit_bytes=8 * 1024 * 1024),
        cost_estimate=pl.CostEstimate(
            flops=0, bytes_accessed=24 * master.size, transcendentals=0
        ),
    )(out_rows, new_master, new_first, new_second)
    shape = master.shape
    return (out_rows, new_master.reshape(shape), new_first.reshape(shape), new_second.reshape(shape))


VMEM_BYTES = 46 * 1024 * 1024


def step(*arrays):
    slots = lax.axis_size("slot")
    weights, fwd_rows = arrays[3], arrays[10]
    owned = weights.shape[2] // slots
    cap = 2 * fwd_rows.shape[0] // slots
    fits = owned % 8 == 0 and cap % 16 == 0 and lax.axis_size("hid") == 4
    fits = fits and weights.shape[3] == 4 * fwd_rows.shape[1] and weights.shape[3] % 1024 == 0
    fits = fits and arrays[4].shape[1] % ROW_STEP == 0
    return (fused_shards if fits else shards)(*arrays)


def solution(mesh):
    return jax.shard_map(
        step,
        mesh=mesh,
        in_specs=(
            P(None, None, "hid", "slot"),
            P(None, None, "hid", "slot"),
            P(None, None, "hid", "slot"),
            P("slot", None, "hid", None),
            P("slot", None, None),
            P("slot", None, None),
            P("slot", None),
            P("slot", None),
            P(),
            P(),
            P("slot", "hid"),
            P("slot", None),
        ),
        out_specs=(
            P("slot", "hid"),
            P(None, None, "hid", "slot"),
            P(None, None, "hid", "slot"),
            P(None, None, "hid", "slot"),
        ),
        check_vma=False,
    )
```
